32 devices in a mesh: grp: 8 (over y, x, core), blk: 4 (over z).
Axes of the slice: x: 2, y: 2, z: 4, core: 2. Of those that a mesh axis runs over, the one named last changes fastest.
Arguments:
- patches: bfloat16 [256, 64, 1152], P(('grp', 'blk')), may hold values from -200 to 200
- probe: bfloat16 [1152], replicated, may hold values from -4 to 4
- w_key: bfloat16 [1152, 1152], P('grp'), may hold values from -0.125 to 1.125
- w_value: bfloat16 [1152, 1152], P('grp'), may hold values from -0.1875 to 0.1875
- w_out: bfloat16 [1152, 1152], P('grp'), may hold values from -0.1875 to 0.1875
- texts: bfloat16 [256, 1152], P(('grp', 'blk')), may hold values from -4 to 4
Outputs:
- grad_image: float32 [256, 1152], P(('grp', 'blk'))
- grad_text: float32 [256, 1152], P(('grp', 'blk'))
The draws below stay inside these ranges and needn't reach their ends.
All inputs are finite; a program needn't handle non-finite values.
Results may differ from the reference program's by a relative error of at most 0.0095.
Values may be sent and summed in bfloat16 or wider, within the bound.
No kernel may reach another device: no remote copies, remote signals or barrier semaphores. Data moves between devices by JAX's collectives and lax.ppermute only.
A program may use at most 64 MiB of HBM per device.

```python
import math
import jax
import jax.numpy as jnp
from jax import lax

D = 1152
HEADS = 16
PATCH = 64
GROUP = 32
BATCH = 256
N_GRP = 8


def probe_vector(key):
    return jnp.clip(jax.random.normal(jax.random.fold_in(key, 101), (D,), jnp.float32), -4.0, 4.0)


def log_spread(key, count, lower, upper):
    return jnp.exp(jax.random.uniform(key, (count,), jnp.float32, jnp.log(lower), jnp.log(upper)))


def draw_probe(key, part):
    shared = probe_vector(key)
    return shared.astype(jnp.bfloat16)


def draw_patches(key, part):
    key = jax.random.fold_in(key, 2)
    streams = jax.random.split(key, 3)
    column = log_spread(streams[0], D, 0.3, 3.0)
    image_scale = log_spread(streams[1], BATCH, 0.05, 0.5)
    base = jnp.clip(jax.random.normal(streams[2], (BATCH, PATCH, D), jnp.float32), -4.0, 4.0)
    field = base * image_scale[:, None, None] * column[None, None, :]
    return field.astype(jnp.bfloat16)


def draw_w_key(key, part):
    key = jax.random.fold_in(key, 3)
    noise = jax.random.normal(key, (D, D), jnp.float32) / jnp.sqrt(jnp.float32(D))
    noise = jnp.clip(noise, -0.125, 0.125)
    return (jnp.eye(D, dtype=jnp.float32) + noise).astype(jnp.bfloat16)


def draw_texts(key, part):
    key = jax.random.fold_in(key, 4)
    streams = jax.random.split(key, 3)
    column = log_spread(streams[0], D, 0.3, 3.0)
    row_scale = log_spread(streams[1], BATCH, 0.02, 0.2)
    base = jnp.clip(jax.random.normal(streams[2], (BATCH, D), jnp.float32), -4.0, 4.0)
    return (base * row_scale[:, None] * column[None, :]).astype(jnp.bfloat16)


def level_of(key, shape, shards, smallest, top_value):
    def one(position, blocks):
        steps = jax.random.uniform(jax.random.fold_in(jax.random.fold_in(key, 6), position), (blocks,), jnp.float32, smallest / len(shards), top_value / len(shards))
        return jnp.repeat(jnp.exp(steps), shape[position] // blocks).reshape((-1,) + (1,) * (len(shape) - position - 1))

    level = one(*shards[0])
    for cut in shards[1:]:
        level = level * one(*cut)
    return level


def normal_values(key, dims, scale, most, shards=(), kind=jnp.bfloat16):
    array = scale * jax.random.normal(key, dims, jnp.float32)
    if shards:
        array = array * level_of(key, dims, shards, -0.22, 0.18)
    return jnp.clip(array, -most, most).astype(kind)


def setup_inputs(seed: int = 0) -> dict:
    seeds = jax.random.split(jax.random.key(seed), 7)
    return {
        "patches": draw_patches(jax.random.fold_in(seeds[6], 71), 0),
        "probe": draw_probe(jax.random.fold_in(seeds[6], 71), 0),
        "w_key": draw_w_key(jax.random.fold_in(seeds[6], 71), 0),
        "w_value": normal_values(seeds[3], (D, D), D ** -0.5, 0.1875, ((0, 8),)),
        "w_out": normal_values(seeds[4], (D, D), D ** -0.5, 0.1875, ((0, 8),)),
        "texts": draw_texts(jax.random.fold_in(seeds[6], 71), 0),
    }


def head_table():
    head_size = D // HEADS
    owner = jnp.arange(D, dtype=jnp.int32) // head_size
    return (owner[:, None] == jnp.arange(HEADS, dtype=jnp.int32)[None, :]).astype(jnp.float32)

def unit_rows(values):
    inverse = lax.rsqrt(lax.optimization_barrier(jnp.sum(values * values, axis=1, keepdims=True)) + 1e-06)
    return (values * inverse, inverse)

def chain_back(grad_unit, unit_f, inverse):
    inner = lax.optimization_barrier(jnp.sum(unit_f * grad_unit, axis=1, keepdims=True))
    return (grad_unit - unit_f * inner) * inverse

def reference(patches, probe, w_key, w_value, w_out, texts):
    head_size = D // HEADS
    scaling = 1.0 / math.sqrt(head_size)
    query_table = head_table() * probe.astype(jnp.float32)[:, None]
    probe_keys = jnp.dot(w_key.astype(jnp.float32), query_table, precision=lax.Precision.HIGHEST)
    split_values = w_value.astype(jnp.float32).reshape(D, HEADS, head_size)
    image_groups = patches.reshape(N_GRP, GROUP, PATCH, D)
    text_groups = texts.reshape(N_GRP, GROUP, D)
    diagonal = jnp.eye(GROUP, dtype=jnp.float32)

    def one_group(pair):
        images, words = pair
        field = images.astype(jnp.float32)
        scores = jnp.einsum('rpd,dh->rph', field, probe_keys, precision=lax.Precision.HIGHEST) * scaling
        top = lax.optimization_barrier(jnp.max(scores, axis=1, keepdims=True))
        expo = jnp.exp(scores - top)
        weights = expo / lax.optimization_barrier(jnp.sum(expo, axis=1, keepdims=True))
        mixed = jnp.einsum('rph,rpd->rhd', weights, field, precision=lax.Precision.HIGHEST)
        pooled = jnp.einsum('rhd,dhk->rhk', mixed, split_values, precision=lax.Precision.HIGHEST)
        pooled = pooled.reshape(GROUP, D).astype(jnp.bfloat16)
        embed = jnp.dot(pooled, w_out, preferred_element_type=jnp.float32)
        unit_image, inverse_image = unit_rows(embed)
        unit_image_b = unit_image.astype(jnp.bfloat16)
        unit_text, inverse_text = unit_rows(words.astype(jnp.float32))
        unit_text_b = unit_text.astype(jnp.bfloat16)
        logits = 10.0 * lax.dot_general(unit_image_b, unit_text_b, (((1,), (1,)), ((), ())), preferred_element_type=jnp.float32) - 2.0
        slopes = (jax.nn.sigmoid(logits) - diagonal).astype(jnp.bfloat16)
        grad_unit_image = 10.0 * jnp.dot(slopes, unit_text_b, preferred_element_type=jnp.float32)
        grad_unit_text = 10.0 * lax.dot_general(slopes, unit_image_b, (((0,), (0,)), ((), ())), preferred_element_type=jnp.float32)
        return (chain_back(grad_unit_image, unit_image, inverse_image), chain_back(grad_unit_text, unit_text, inverse_text))
    grad_image, grad_text = lax.map(one_group, (image_groups, text_groups))
    return (grad_image.reshape(BATCH, D), grad_text.reshape(BATCH, D))
```

```python
import functools
import math

import jax
import jax.numpy as jnp
from jax import lax
from jax.experimental import pallas as pl
from jax.experimental.pallas import tpu as pltpu
from jax.sharding import PartitionSpec as P

HEADS = 16
CORES = 2
F32 = jnp.float32
BF16 = jnp.bfloat16


def struct(shape, dtype):
    return jax.ShapeDtypeStruct(shape, dtype)


def call(body, out, *args, scratch=(), space=pltpu.VMEM):
    return pl.pallas_call(
        body,
        out_shape=out,
        in_specs=[pl.BlockSpec(memory_space=space)] * len(args),
        scratch_shapes=scratch,
        compiler_params=pltpu.CompilerParams(vmem_limit_bytes=24 * 2**20),
    )(*args)


def nt(left, right):
    return lax.dot_general(left, right, (((1,), (1,)), ((), ())), preferred_element_type=F32)


def nn(left, right):
    return jnp.dot(left, right, preferred_element_type=F32)


def unit_rows(values):
    inverse = lax.rsqrt(jnp.sum(values * values, axis=1, keepdims=True) + 1e-06)
    return values * inverse, inverse


def chain_back(grad_unit, unit_f, inverse):
    inner = jnp.sum(unit_f * grad_unit, axis=1, keepdims=True)
    return (grad_unit - unit_f * inner) * inverse


def slopes_of(left, right, place):
    logits = 10.0 * nt(left, right) - 2.0
    row = lax.broadcasted_iota(jnp.int32, logits.shape, 0)
    column = lax.broadcasted_iota(jnp.int32, logits.shape, 1)
    target = jnp.where(row + place == column, 1.0, 0.0)
    return (jax.nn.sigmoid(logits) - target).astype(BF16)


def split_terms(values):
    high = values.astype(BF16)
    rest = values - high.astype(F32)
    middle = rest.astype(BF16)
    return high, middle, (rest - middle.astype(F32)).astype(BF16)


def prepare_kernel(
    probe_hbm, w_key_hbm, w_value_hbm, out_ref, probe, w_key, w_value, sems
):
    part, width = w_key.shape
    devices, rows, _ = out_ref.shape
    copies = [
        pltpu.make_async_copy(source, target, sems.at[i])
        for i, (source, target) in enumerate(
            [(probe_hbm, probe), (w_key_hbm, w_key), (w_value_hbm, w_value)]
        )
    ]
    for copy in copies:
        copy.start()
    head = lax.broadcasted_iota(jnp.int32, (HEADS, width), 0)
    first = lax.broadcasted_iota(jnp.int32, (HEADS, width), 1) - head * (width // HEADS)
    inside = (first >= 0) & (first < width // HEADS)
    copies[0].wait()
    copies[1].wait()
    table = jnp.where(inside, probe[...].astype(F32).reshape(1, width), 0.0).astype(BF16)
    keys = [
        term[h * rows : (h + 1) * rows]
        for term in split_terms(nt(table, w_key[...]))
        for h in range(HEADS // rows)
    ]
    copies[2].wait()
    for k in range(devices):
        columns = w_value[:, k * part : (k + 1) * part]
        pieces = [columns[j * rows : (j + 1) * rows] for j in range(part // rows)]
        out_ref[k] = jnp.concatenate(pieces + keys, axis=1)


def shard_kernel(parts_ref, w_out_ref, out_ref):
    devices, rows, _ = parts_ref.shape
    part, width = w_out_ref.shape
    packed = part // rows * part
    out_ref[:devices, :, :packed] = parts_ref[:, :, :packed]
    out_ref[devices:, :, :width] = w_out_ref[...].reshape(part // rows, rows, width)


def attend_kernel(images, scaling, x_ref, parts_ref, *refs):
    outs, (table, every) = refs[:-2], refs[-2:]
    x = x_ref[...]
    width = x.shape[1]
    patches = x.shape[0] // images
    devices, rows, length = parts_ref.shape
    part = width // devices
    pieces = table.shape[0] // rows
    for j in range(pieces):
        first = length - (pieces - j) * part
        for k in range(devices):
            table[j * rows : (j + 1) * rows, k * part : (k + 1) * part] = parts_ref[
                k, :, first : first + part
            ]
    parts = nt(table[...], x)
    scores = (parts[:HEADS] + parts[HEADS : 2 * HEADS] + parts[2 * HEADS :]) * scaling
    image = lax.broadcasted_iota(jnp.int32, (images, x.shape[0]), 0)
    first = lax.broadcasted_iota(jnp.int32, (images, x.shape[0]), 1) - image * patches
    own = (first >= 0) & (first < patches)
    spread = jnp.where(own[None], scores[:, None, :], -jnp.inf)
    expo = jnp.exp(spread - jnp.max(spread, axis=2, keepdims=True))
    weights = expo / jnp.sum(expo, axis=2, keepdims=True)
    weights = weights.reshape(HEADS * images, x.shape[0])
    high = weights.astype(BF16)
    low = (weights - high.astype(F32)).astype(BF16)
    mixed = nn(jnp.concatenate([high, low], axis=0), x)
    mixed = (mixed[: HEADS * images] + mixed[HEADS * images :]).astype(BF16)
    every[...] = mixed.reshape(every.shape)
    chip = lax.axis_index("grp") // CORES
    for m, out_ref in enumerate(outs):
        out_ref[...] = every[chip ^ m]


def project_kernel(images, chips, *refs):
    mixed_refs, (parts_ref, w_out_ref, other_ref) = refs[:chips], refs[chips : chips + 3]
    out_refs, w_value = refs[chips + 3 : -1], refs[-1]
    _, rows, width = mixed_refs[0].shape
    devices = parts_ref.shape[0]
    part = w_out_ref.shape[0]
    heads = rows // images
    core = lax.rem(lax.axis_index("grp"), CORES)
    head = lax.broadcasted_iota(jnp.int32, (chips, images, part), 2)
    embed = jnp.zeros((chips * images, width), F32)
    for s, columns in enumerate((parts_ref, other_ref)):
        for k in range(devices):
            for j in range(part // rows):
                w_value[s, k * part + j * rows : k * part + (j + 1) * rows] = columns[
                    k, :, j * part : (j + 1) * part
                ]
        shard = core if s == 0 else 1 - core
        mixed = jnp.concatenate([ref[shard] for ref in mixed_refs], axis=0)
        every = nn(mixed, w_value[s]).reshape(chips, heads, images, part)
        pooled = every[:, 0]
        for h in range(1, heads):
            pooled = jnp.where(head >= h * (part // heads), every[:, h], pooled)
        pooled = pooled.reshape(chips * images, part).astype(BF16)
        rows_out = w_out_ref[...]
        if s == 1:
            rows_out = other_ref[devices:, :, :width].reshape(part, width)
        embed = embed + nn(pooled, rows_out)
    for m, out_ref in enumerate(out_refs):
        out_ref[...] = embed[m * images : (m + 1) * images].astype(BF16)


def unit_image_kernel(chips, *refs):
    text_ref, unit_ref, inverse_ref, both_ref = refs[chips:]
    embed = refs[0][...].astype(F32)
    for ref in refs[1:chips]:
        embed = embed + ref[...].astype(F32)
    unit, inverse = unit_rows(embed)
    unit_ref[...] = unit
    inverse_ref[...] = jnp.broadcast_to(inverse, inverse_ref.shape)
    for k in range(both_ref.shape[0]):
        both_ref[k, 0] = unit.astype(BF16)
        both_ref[k, 1] = text_ref[...]


def grads_kernel(unit_ref, inverse_ref, text_ref, both_ref, grad_image_ref, grad_text_ref):
    blocks, _, images, width = both_ref.shape
    place = lax.axis_index("blk") * images
    every = both_ref[...].astype(F32)
    all_images = every[:, 0].reshape(blocks * images, width).astype(BF16)
    all_texts = every[:, 1].reshape(blocks * images, width)
    words = unit_rows(all_texts)[0].astype(BF16)
    unit = unit_ref[...]
    slopes = slopes_of(unit.astype(BF16), words, place)
    grad_image_ref[...] = chain_back(10.0 * nn(slopes, words), unit, inverse_ref[:, :1])
    unit, inverse = unit_rows(text_ref[...].astype(F32))
    slopes = slopes_of(unit.astype(BF16), all_images, place)
    grad_text_ref[...] = chain_back(10.0 * nn(slopes, all_images), unit, inverse)


def swap(array, axis):
    return lax.all_to_all(array, axis, 0, 0, tiled=True)


def exchange(array, devices, flip):
    return lax.ppermute(array, "grp", [(i, i ^ flip) for i in range(devices)])


def exchange_chips(arrays, devices):
    return [array if m == 0 else exchange(array, devices, m * CORES) for m, array in enumerate(arrays)]


def local(patches, probe, w_key, w_value, w_out, texts):
    images, patch_count, width = patches.shape
    devices = lax.axis_size("grp")
    blocks = lax.axis_size("blk")
    part = w_key.shape[0]
    heads = HEADS // devices
    scaling = 1.0 / math.sqrt(width // HEADS)
    flat = patches.reshape(images * patch_count, width)

    rows = heads * images
    packed = part // rows * part
    chips = devices // CORES
    parts = call(
        prepare_kernel,
        struct((devices, rows, packed + 3 * HEADS // rows * part), BF16),
        *[pltpu.with_memory_space_constraint(a, pltpu.HBM) for a in (probe, w_key, w_value)],
        scratch=[
            pltpu.VMEM(probe.shape, BF16),
            pltpu.VMEM(w_key.shape, BF16),
            pltpu.VMEM(w_value.shape, BF16),
            pltpu.SemaphoreType.DMA((3,)),
        ],
        space=pltpu.HBM,
    )
    parts = swap(parts, "grp")
    shard = call(
        shard_kernel,
        struct((devices + part // rows, rows, max(packed, width)), BF16),
        parts,
        w_out,
    )
    other = exchange(shard, devices, 1)
    mixed = call(
        functools.partial(attend_kernel, images, scaling),
        [struct((CORES, rows, width), BF16)] * chips,
        flat,
        parts,
        scratch=[
            pltpu.VMEM((3 * HEADS, width), BF16),
            pltpu.VMEM((chips, CORES, rows, width), BF16),
        ],
    )
    partial_embed = call(
        functools.partial(project_kernel, images, chips),
        [struct((images, width), BF16)] * chips,
        *exchange_chips(mixed, devices),
        parts,
        w_out,
        other,
        scratch=[pltpu.VMEM((CORES, width, part), BF16)],
    )
    unit, inverse, both = call(
        functools.partial(unit_image_kernel, chips),
        (
            struct((images, width), F32),
            struct((images, 128), F32),
            struct((blocks, 2, images, width), BF16),
        ),
        *exchange_chips(partial_embed, devices),
        texts,
    )
    return call(
        grads_kernel,
        (struct((images, width), F32), struct((images, width), F32)),
        unit,
        inverse,
        texts,
        swap(both, "blk"),
    )


def solution(mesh):
    in_specs = (
        P(("grp", "blk"), None, None),
        P(),
        P("grp", None),
        P("grp", None),
        P("grp", None),
        P(("grp", "blk"), None),
    )
    out_specs = (P(("grp", "blk"), None), P(("grp", "blk"), None))
    return jax.shard_map(local, mesh=mesh, in_specs=in_specs, out_specs=out_specs, check_vma=False)
```

```python
import functools
import math

import jax
import jax.numpy as jnp
from jax import lax
from jax.experimental import pallas as pl
from jax.experimental.pallas import tpu as pltpu
from jax.sharding import PartitionSpec as P

HEADS = 16
CORES = 2
F32 = jnp.float32
BF16 = jnp.bfloat16


def struct(shape, dtype):
    return jax.ShapeDtypeStruct(shape, dtype)


def call(body, out, *args, scratch=(), space=pltpu.VMEM):
    return pl.pallas_call(
        body,
        out_shape=out,
        in_specs=[pl.BlockSpec(memory_space=space)] * len(args),
        scratch_shapes=scratch,
        compiler_params=pltpu.CompilerParams(vmem_limit_bytes=24 * 2**20),
    )(*args)


def nt(left, right):
    return lax.dot_general(left, right, (((1,), (1,)), ((), ())), preferred_element_type=F32)


def nn(left, right):
    return jnp.dot(left, right, preferred_element_type=F32)


def unit_rows(values):
    inverse = lax.rsqrt(jnp.sum(values * values, axis=1, keepdims=True) + 1e-06)
    return values * inverse, inverse


def chain_back(grad_unit, unit_f, inverse):
    inner = jnp.sum(unit_f * grad_unit, axis=1, keepdims=True)
    return (grad_unit - unit_f * inner) * inverse


def slopes_of(left, right):
    logits = 10.0 * nt(left, right) - 2.0
    row = lax.broadcasted_iota(jnp.int32, logits.shape, 0)
    column = lax.broadcasted_iota(jnp.int32, logits.shape, 1)
    target = jnp.where(row == column, 1.0, 0.0)
    return (jax.nn.sigmoid(logits) - target).astype(BF16)


def split_terms(values):
    high = values.astype(BF16)
    rest = values - high.astype(F32)
    middle = rest.astype(BF16)
    return high, middle, (rest - middle.astype(F32)).astype(BF16)


def chip_and_core():
    place = lax.axis_index("grp")
    return place // CORES, lax.rem(place, CORES)


def prepare_kernel(
    probe_hbm, w_key_hbm, w_value_hbm, keys_ref, table_ref, blocks_ref, probe, w_key, w_value, sems
):
    part, width = w_key.shape
    chips, rows, _ = blocks_ref.shape
    copies = [
        pltpu.make_async_copy(source, target, sems.at[i])
        for i, (source, target) in enumerate(
            [(probe_hbm, probe), (w_key_hbm, w_key), (w_value_hbm, w_value)]
        )
    ]
    for copy in copies:
        copy.start()
    head = lax.broadcasted_iota(jnp.int32, (HEADS, width), 0)
    first = lax.broadcasted_iota(jnp.int32, (HEADS, width), 1) - head * (width // HEADS)
    inside = (first >= 0) & (first < width // HEADS)
    copies[0].wait()
    table = jnp.where(inside, probe[...].astype(F32).reshape(1, width), 0.0).astype(BF16)
    table_ref[...] = table
    copies[1].wait()
    keys_ref[...] = nt(table, w_key[...])
    copies[2].wait()
    wide = width // chips
    for q in range(chips):
        columns = w_value[:, q * wide : (q + 1) * wide]
        pieces = [columns[j * rows : (j + 1) * rows] for j in range(part // rows)]
        blocks_ref[q] = jnp.concatenate(pieces, axis=1)


def keys_kernel(keys_ref, table_ref, blocks_ref, other_ref, *out_refs):
    _, rows, packed = blocks_ref.shape
    chip, core = chip_and_core()
    own, other = keys_ref[...], nt(table_ref[...], other_ref[...])
    keys = [jnp.where(core == 0, own, other), jnp.where(core == 0, other, own)]
    keys = [
        term[h * rows : (h + 1) * rows]
        for term in split_terms(jnp.concatenate(keys, axis=1))
        for h in range(HEADS // rows)
    ]
    keys = jnp.concatenate(keys, axis=1)
    for m, out_ref in enumerate(out_refs):
        out_ref[:, :packed] = blocks_ref[chip ^ m]
        out_ref[:, packed:] = keys


def shard_kernel(chips, *refs):
    w_out_ref, out_ref = refs[chips:]
    _, rows, length = out_ref.shape
    part, width = w_out_ref.shape
    for m in range(chips):
        out_ref[m] = refs[m][:, :length]
    fit = length // width
    for j in range(part // rows):
        first = j % fit * width
        out_ref[chips + j // fit, :, first : first + width] = w_out_ref[j * rows : (j + 1) * rows]


def attend_kernel(images, scaling, chips, x_ref, *refs):
    parts, outs, (placed, table, every) = refs[:chips], refs[chips:-3], refs[-3:]
    x = x_ref[...]
    width = x.shape[1]
    patches = x.shape[0] // images
    rows, length = parts[0].shape
    wide = width // chips
    pieces = table.shape[0] // rows
    chip, _ = chip_and_core()
    for m in range(chips):
        placed[chip ^ m] = parts[m][:, length - pieces * wide :]
    for j in range(pieces):
        for q in range(chips):
            table[j * rows : (j + 1) * rows, q * wide : (q + 1) * wide] = placed[
                q, :, j * wide : (j + 1) * wide
            ]
    parts = nt(table[...], x)
    scores = (parts[:HEADS] + parts[HEADS : 2 * HEADS] + parts[2 * HEADS :]) * scaling
    image = lax.broadcasted_iota(jnp.int32, (images, x.shape[0]), 0)
    first = lax.broadcasted_iota(jnp.int32, (images, x.shape[0]), 1) - image * patches
    own = (first >= 0) & (first < patches)
    spread = jnp.where(own[None], scores[:, None, :], -jnp.inf)
    expo = jnp.exp(spread - jnp.max(spread, axis=2, keepdims=True))
    weights = expo / jnp.sum(expo, axis=2, keepdims=True)
    weights = weights.reshape(HEADS * images, x.shape[0])
    high = weights.astype(BF16)
    low = (weights - high.astype(F32)).astype(BF16)
    mixed = nn(jnp.concatenate([high, low], axis=0), x)
    mixed = (mixed[: HEADS * images] + mixed[HEADS * images :]).astype(BF16)
    every[...] = mixed.reshape(every.shape)
    for m, out_ref in enumerate(outs):
        out_ref[...] = every[chip ^ m]


def project_kernel(images, chips, *refs):
    mixed_refs, parts = refs[:chips], refs[chips : 2 * chips]
    w_out_ref, other_ref = refs[2 * chips : 2 * chips + 2]
    out_refs, w_value = refs[2 * chips + 2 : -1], refs[-1]
    _, rows, width = mixed_refs[0].shape
    part = w_out_ref.shape[0]
    heads = rows // images
    chip, core = chip_and_core()
    for m in range(chips):
        for c, source in enumerate((parts[m], other_ref.at[m])):
            place = core if c == 0 else 1 - core
            for t in range(CORES):
                for j in range(part // rows):
                    first = (j * CORES + t) * part
                    w_value[t, chip ^ m, place, j * rows : (j + 1) * rows] = source[
                        :, first : first + part
                    ]
    fit = other_ref.shape[2] // width
    outs = [
        other_ref[chips + j // fit, :, j % fit * width : (j % fit + 1) * width]
        for j in range(part // rows)
    ]
    head = lax.broadcasted_iota(jnp.int32, (chips, images, part), 2)
    embed = jnp.zeros((chips * images, width), F32)
    for shard, rows_out in ((core, w_out_ref[...]), (1 - core, jnp.concatenate(outs, axis=0))):
        mixed = jnp.concatenate([ref[shard] for ref in mixed_refs], axis=0)
        columns = w_value[shard].reshape(width, part)
        every = nn(mixed, columns).reshape(chips, heads, images, part)
        pooled = every[:, 0]
        for h in range(1, heads):
            pooled = jnp.where(head >= h * (part // heads), every[:, h], pooled)
        pooled = pooled.reshape(chips * images, part).astype(BF16)
        embed = embed + nn(pooled, rows_out)
    for m, out_ref in enumerate(out_refs):
        out_ref[...] = embed[m * images : (m + 1) * images].astype(BF16)


def unit_text_kernel(blocks, *refs):
    words_ref, unit_ref, inverse_ref = refs[blocks:]
    images = unit_ref.shape[0]
    texts = jnp.concatenate([ref[...].astype(F32) for ref in refs[:blocks]], axis=0)
    units, inverses = unit_rows(texts)
    words_ref[...] = units.astype(BF16)
    unit_ref[...] = units[:images]
    inverse_ref[...] = jnp.broadcast_to(inverses[:images], inverse_ref.shape)


def unit_image_kernel(chips, *refs):
    unit_ref, inverse_ref, rounded_ref = refs[chips + 1 :]
    embed = refs[0][...].astype(F32)
    for ref in refs[1:chips]:
        embed = embed + ref[...].astype(F32)
    unit, inverse = unit_rows(embed)
    unit_ref[...] = unit
    inverse_ref[...] = jnp.broadcast_to(inverse, inverse_ref.shape)
    rounded_ref[...] = unit.astype(BF16)


def grad_kernel(unit_ref, inverse_ref, *refs):
    others = [ref[...].astype(F32) for ref in refs[:-1]]
    others = jnp.concatenate(others, axis=0).astype(BF16)
    unit = unit_ref[...]
    slopes = slopes_of(unit.astype(BF16), others)
    refs[-1][...] = chain_back(10.0 * nn(slopes, others), unit, inverse_ref[:, :1])


def exchange(array, devices, flip, axis="grp"):
    return lax.ppermute(array, axis, [(i, i ^ flip) for i in range(devices)])


def all_blocks(array, blocks):
    return [array] + [
        lax.ppermute(array, "blk", [(i, (i + by) % blocks) for i in range(blocks)])
        for by in range(1, blocks)
    ]


def exchange_chips(arrays, devices):
    return [array if m == 0 else exchange(array, devices, m * CORES) for m, array in enumerate(arrays)]


def local(patches, probe, w_key, w_value, w_out, texts):
    images, patch_count, width = patches.shape
    devices = lax.axis_size("grp")
    blocks = lax.axis_size("blk")
    part = w_key.shape[0]
    heads = HEADS // devices
    scaling = 1.0 / math.sqrt(width // HEADS)
    flat = patches.reshape(images * patch_count, width)

    rows = heads * images
    chips = devices // CORES
    wide = CORES * part
    packed = part // rows * wide
    fit = packed // width

    keys, table, columns = call(
        prepare_kernel,
        (
            struct((HEADS, part), F32),
            struct((HEADS, width), BF16),
            struct((chips, rows, packed), BF16),
        ),
        *[pltpu.with_memory_space_constraint(a, pltpu.HBM) for a in (probe, w_key, w_value)],
        scratch=[
            pltpu.VMEM(probe.shape, BF16),
            pltpu.VMEM(w_key.shape, BF16),
            pltpu.VMEM(w_value.shape, BF16),
            pltpu.SemaphoreType.DMA((3,)),
        ],
        space=pltpu.HBM,
    )
    parts = call(
        keys_kernel,
        [struct((rows, packed + 3 * HEADS // rows * wide), BF16)] * chips,
        keys,
        table,
        columns,
        exchange(w_key, devices, 1),
    )
    parts = exchange_chips(parts, devices)
    shard = call(
        functools.partial(shard_kernel, chips),
        struct((chips + pl.cdiv(part // rows, fit), rows, packed), BF16),
        *parts,
        w_out,
    )
    other = exchange(shard, devices, 1)
    mixed = call(
        functools.partial(attend_kernel, images, scaling, chips),
        [struct((CORES, rows, width), BF16)] * chips,
        flat,
        *parts,
        scratch=[
            pltpu.VMEM((chips, rows, 3 * HEADS // rows * wide), BF16),
            pltpu.VMEM((3 * HEADS, width), BF16),
            pltpu.VMEM((chips, CORES, rows, width), BF16),
        ],
    )
    partial_embed = call(
        functools.partial(project_kernel, images, chips),
        [struct((images, width), BF16)] * chips,
        *exchange_chips(mixed, devices),
        *parts,
        w_out,
        other,
        scratch=[pltpu.VMEM((CORES, chips, CORES, part, part), BF16)],
    )
    row, column = struct((images, width), F32), struct((images, 128), F32)
    words, unit_text, inverse_text = call(
        functools.partial(unit_text_kernel, blocks),
        (struct((blocks * images, width), BF16), row, column),
        *all_blocks(texts, blocks),
    )
    unit, inverse, rounded = call(
        functools.partial(unit_image_kernel, chips),
        (row, column, struct((images, width), BF16)),
        *exchange_chips(partial_embed, devices),
        inverse_text,
    )
    all_images = [rounded] + [exchange(rounded, blocks, m, "blk") for m in range(1, blocks)]
    grad_image = call(grad_kernel, row, unit, inverse, words)
    grad_text = call(grad_kernel, row, unit_text, inverse_text, *all_images)
    return grad_image, grad_text


def solution(mesh):
    in_specs = (
        P(("grp", "blk"), None, None),
        P(),
        P("grp", None),
        P("grp", None),
        P("grp", None),
        P(("grp", "blk"), None),
    )
    out_specs = (P(("grp", "blk"), None), P(("grp", "blk"), None))
    return jax.shard_map(local, mesh=mesh, in_specs=in_specs, out_specs=out_specs, check_vma=False)
```

```python
import functools
import math

import jax
import jax.numpy as jnp
from jax import lax
from jax.experimental import pallas as pl
from jax.experimental.pallas import tpu as pltpu
from jax.sharding import PartitionSpec as P

HEADS = 16
CORES = 2
F32 = jnp.float32
BF16 = jnp.bfloat16


def struct(shape, dtype):
    return jax.ShapeDtypeStruct(shape, dtype)


def call(body, out, *args, scratch=(), space=pltpu.VMEM):
    return pl.pallas_call(
        body,
        out_shape=out,
        in_specs=[pl.BlockSpec(memory_space=space)] * len(args),
        scratch_shapes=scratch,
        compiler_params=pltpu.CompilerParams(vmem_limit_bytes=24 * 2**20),
    )(*args)


def nt(left, right):
    return lax.dot_general(left, right, (((1,), (1,)), ((), ())), preferred_element_type=F32)


def nn(left, right):
    return jnp.dot(left, right, preferred_element_type=F32)


def unit_rows(values):
    inverse = lax.rsqrt(jnp.sum(values * values, axis=1, keepdims=True) + 1e-06)
    return values * inverse, inverse


def chain_back(grad_unit, unit_f, inverse):
    inner = jnp.sum(unit_f * grad_unit, axis=1, keepdims=True)
    return (grad_unit - unit_f * inner) * inverse


def slopes_of(left, right):
    logits = 10.0 * nt(left, right) - 2.0
    row = lax.broadcasted_iota(jnp.int32, logits.shape, 0)
    column = lax.broadcasted_iota(jnp.int32, logits.shape, 1)
    target = jnp.where(row == column, 1.0, 0.0)
    return (jax.nn.sigmoid(logits) - target).astype(BF16)


def split_terms(values):
    high = values.astype(BF16)
    rest = values - high.astype(F32)
    middle = rest.astype(BF16)
    return high, middle, (rest - middle.astype(F32)).astype(BF16)


def flips(chips):
    return [0, *range(chips - 1, 0, -1)]


def chip_and_core():
    place = lax.axis_index("grp")
    return place // CORES, lax.rem(place, CORES)


def prepare_kernel(
    probe_hbm, w_key_hbm, w_value_hbm, keys_ref, table_ref, blocks_ref, probe, w_key, w_value, sems
):
    part, width = w_key.shape
    chips, rows, _ = blocks_ref.shape
    copies = [
        pltpu.make_async_copy(source, target, sems.at[i])
        for i, (source, target) in enumerate(
            [(probe_hbm, probe), (w_key_hbm, w_key), (w_value_hbm, w_value)]
        )
    ]
    for copy in copies:
        copy.start()
    head = lax.broadcasted_iota(jnp.int32, (HEADS, width), 0)
    first = lax.broadcasted_iota(jnp.int32, (HEADS, width), 1) - head * (width // HEADS)
    inside = (first >= 0) & (first < width // HEADS)
    copies[0].wait()
    table = jnp.where(inside, probe[...].astype(F32).reshape(1, width), 0.0).astype(BF16)
    table_ref[...] = table
    copies[1].wait()
    keys_ref[...] = nt(table, w_key[...])
    copies[2].wait()
    wide = width // chips
    for q in range(chips):
        columns = w_value[:, q * wide : (q + 1) * wide]
        pieces = [columns[j * rows : (j + 1) * rows] for j in range(part // rows)]
        blocks_ref[q] = jnp.concatenate(pieces, axis=1)


def keys_kernel(keys_ref, table_ref, blocks_ref, other_ref, *out_refs):
    _, rows, packed = blocks_ref.shape
    chip, core = chip_and_core()
    own, other = keys_ref[...], nt(table_ref[...], other_ref[...])
    keys = [jnp.where(core == 0, own, other), jnp.where(core == 0, other, own)]
    keys = [
        term[h * rows : (h + 1) * rows]
        for term in split_terms(jnp.concatenate(keys, axis=1))
        for h in range(HEADS // rows)
    ]
    keys = jnp.concatenate(keys, axis=1)
    for m, out_ref in zip(flips(len(out_refs)), out_refs):
        out_ref[:, :packed] = blocks_ref[chip ^ m]
        out_ref[:, packed:] = keys


def shard_kernel(chips, *refs):
    w_out_ref, out_ref = refs[chips:]
    _, rows, length = out_ref.shape
    part, width = w_out_ref.shape
    for i in range(chips):
        out_ref[i] = refs[i][:, :length]
    fit = length // width
    for j in range(part // rows):
        first = j % fit * width
        out_ref[chips + j // fit, :, first : first + width] = w_out_ref[j * rows : (j + 1) * rows]


def attend_kernel(images, scaling, chips, x_ref, *refs):
    parts, outs, (placed, table, every) = refs[:chips], refs[chips:-3], refs[-3:]
    x = x_ref[...]
    width = x.shape[1]
    patches = x.shape[0] // images
    rows, length = parts[0].shape
    wide = width // chips
    pieces = table.shape[0] // rows
    chip, _ = chip_and_core()
    for m, part_ref in zip(flips(chips), parts):
        placed[chip ^ m] = part_ref[:, length - pieces * wide :]
    for j in range(pieces):
        for q in range(chips):
            table[j * rows : (j + 1) * rows, q * wide : (q + 1) * wide] = placed[
                q, :, j * wide : (j + 1) * wide
            ]
    parts = nt(table[...], x)
    scores = (parts[:HEADS] + parts[HEADS : 2 * HEADS] + parts[2 * HEADS :]) * scaling
    image = lax.broadcasted_iota(jnp.int32, (images, x.shape[0]), 0)
    first = lax.broadcasted_iota(jnp.int32, (images, x.shape[0]), 1) - image * patches
    own = (first >= 0) & (first < patches)
    spread = jnp.where(own[None], scores[:, None, :], -jnp.inf)
    expo = jnp.exp(spread - jnp.max(spread, axis=2, keepdims=True))
    weights = expo / jnp.sum(expo, axis=2, keepdims=True)
    weights = weights.reshape(HEADS * images, x.shape[0])
    every[...] = nn(weights.astype(BF16), x).astype(BF16).reshape(every.shape)
    for m, out_ref in zip(flips(chips), outs):
        out_ref[...] = every[chip ^ m]


def unpack_kernel(chips, *refs):
    w_out_ref, other_ref, w_value_ref, outs_ref = refs[chips:]
    part, width = w_out_ref.shape
    rows = other_ref.shape[1]
    chip, core = chip_and_core()
    for i, m in enumerate(flips(chips)):
        for c, source in enumerate((refs[i], other_ref.at[i])):
            place = core if (c == 0) == (m == 0) else 1 - core
            for t in range(CORES):
                for j in range(part // rows):
                    first = (j * CORES + t) * part
                    w_value_ref[t, chip ^ m, place, j * rows : (j + 1) * rows] = source[
                        :, first : first + part
                    ]
    outs_ref[core] = w_out_ref[...]
    fit = other_ref.shape[2] // width
    for j in range(part // rows):
        first = j % fit * width
        outs_ref[1 - core, j * rows : (j + 1) * rows] = other_ref[
            chips + j // fit, :, first : first + width
        ]


def project_kernel(images, chips, *refs):
    mixed_refs, (w_value_ref, outs_ref), out_refs = refs[:chips], refs[chips : chips + 2], refs[chips + 2 :]
    _, rows, width = mixed_refs[0].shape
    part = outs_ref.shape[1]
    heads = rows // images
    head = lax.broadcasted_iota(jnp.int32, (chips, images, part), 2)
    embed = jnp.zeros((chips * images, width), F32)
    for t in range(CORES):
        mixed = jnp.concatenate([ref[t] for ref in mixed_refs], axis=0)
        every = nn(mixed, w_value_ref[t].reshape(width, part))
        every = every.reshape(chips, heads, images, part)
        pooled = every[:, 0]
        for h in range(1, heads):
            pooled = jnp.where(head >= h * (part // heads), every[:, h], pooled)
        pooled = pooled.reshape(chips * images, part).astype(BF16)
        embed = embed + nn(pooled, outs_ref[t])
    for i, out_ref in enumerate(out_refs):
        out_ref[...] = embed[i * images : (i + 1) * images].astype(BF16)


def unit_text_kernel(blocks, *refs):
    words_ref, unit_ref, inverse_ref = refs[blocks:]
    images = unit_ref.shape[0]
    texts = jnp.concatenate([ref[...].astype(F32) for ref in refs[:blocks]], axis=0)
    units, inverses = unit_rows(texts)
    words_ref[...] = units.astype(BF16)
    unit_ref[...] = units[:images]
    inverse_ref[...] = jnp.broadcast_to(inverses[:images], inverse_ref.shape)


def unit_image_kernel(chips, *refs):
    unit_ref, inverse_ref, rounded_ref = refs[chips + 1 :]
    embed = refs[0][...].astype(F32)
    for ref in refs[1:chips]:
        embed = embed + ref[...].astype(F32)
    unit, inverse = unit_rows(embed)
    unit_ref[...] = unit
    inverse_ref[...] = jnp.broadcast_to(inverse, inverse_ref.shape)
    rounded_ref[...] = unit.astype(BF16)


def grad_kernel(unit_ref, inverse_ref, *refs):
    others = [ref[...].astype(F32) for ref in refs[:-1]]
    others = jnp.concatenate(others, axis=0).astype(BF16)
    unit = unit_ref[...]
    slopes = slopes_of(unit.astype(BF16), others)
    refs[-1][...] = chain_back(10.0 * nn(slopes, others), unit, inverse_ref[:, :1])


def exchange(array, devices, flip, axis="grp"):
    return lax.ppermute(array, axis, [(i, i ^ flip) for i in range(devices)])


def all_blocks(array, blocks):
    return [array] + [
        lax.ppermute(array, "blk", [(i, (i + by) % blocks) for i in range(blocks)])
        for by in range(1, blocks)
    ]


def exchange_chips(arrays, devices):
    return [
        exchange(array, devices, m * CORES + 1) if m else array
        for m, array in zip(flips(len(arrays)), arrays)
    ]


def local(patches, probe, w_key, w_value, w_out, texts):
    images, patch_count, width = patches.shape
    devices = lax.axis_size("grp")
    blocks = lax.axis_size("blk")
    part = w_key.shape[0]
    heads = HEADS // devices
    scaling = 1.0 / math.sqrt(width // HEADS)
    flat = patches.reshape(images * patch_count, width)

    rows = heads * images
    chips = devices // CORES
    wide = CORES * part
    packed = part // rows * wide
    fit = packed // width

    keys, table, columns = call(
        prepare_kernel,
        (
            struct((HEADS, part), F32),
            struct((HEADS, width), BF16),
            struct((chips, rows, packed), BF16),
        ),
        *[pltpu.with_memory_space_constraint(a, pltpu.HBM) for a in (probe, w_key, w_value)],
        scratch=[
            pltpu.VMEM(probe.shape, BF16),
            pltpu.VMEM(w_key.shape, BF16),
            pltpu.VMEM(w_value.shape, BF16),
            pltpu.SemaphoreType.DMA((3,)),
        ],
        space=pltpu.HBM,
    )
    parts = call(
        keys_kernel,
        [struct((rows, packed + 3 * HEADS // rows * wide), BF16)] * chips,
        keys,
        table,
        columns,
        exchange(w_key, devices, 1),
    )
    parts = exchange_chips(parts, devices)
    mixed = call(
        functools.partial(attend_kernel, images, scaling, chips),
        [struct((CORES, rows, width), BF16)] * chips,
        flat,
        *parts,
        scratch=[
            pltpu.VMEM((chips, rows, 3 * HEADS // rows * wide), BF16),
            pltpu.VMEM((3 * HEADS, width), BF16),
            pltpu.VMEM((chips, CORES, rows, width), BF16),
        ],
    )
    shard = call(
        functools.partial(shard_kernel, chips),
        struct((chips + pl.cdiv(part // rows, fit), rows, packed), BF16),
        *parts,
        w_out,
    )
    w_values, w_outs = call(
        functools.partial(unpack_kernel, chips),
        (
            struct((CORES, chips, CORES, part, part), BF16),
            struct((CORES, part, width), BF16),
        ),
        *parts,
        w_out,
        exchange(shard, devices, 1),
    )
    partial_embed = call(
        functools.partial(project_kernel, images, chips),
        [struct((images, width), BF16)] * chips,
        *exchange_chips(mixed, devices),
        w_values,
        w_outs,
    )
    row, column = struct((images, width), F32), struct((images, 128), F32)
    words, unit_text, inverse_text = call(
        functools.partial(unit_text_kernel, blocks),
        (struct((blocks * images, width), BF16), row, column),
        *all_blocks(texts, blocks),
    )
    unit, inverse, rounded = call(
        functools.partial(unit_image_kernel, chips),
        (row, column, struct((images, width), BF16)),
        *exchange_chips(partial_embed, devices),
        inverse_text,
    )
    all_images = [exchange(rounded, blocks, m, "blk") for m in range(blocks - 1, 0, -1)]
    grad_image = call(grad_kernel, row, unit, inverse, words)
    grad_text = call(grad_kernel, row, unit_text, inverse_text, rounded, *all_images)
    return grad_image, grad_text


def solution(mesh):
    in_specs = (
        P(("grp", "blk"), None, None),
        P(),
        P("grp", None),
        P("grp", None),
        P("grp", None),
        P(("grp", "blk"), None),
    )
    out_specs = (P(("grp", "blk"), None), P(("grp", "blk"), None))
    return jax.shard_map(local, mesh=mesh, in_specs=in_specs, out_specs=out_specs, check_vma=False)
```

```python
import functools
import math

import jax
import jax.numpy as jnp
from jax import lax
from jax.experimental import pallas as pl
from jax.experimental.pallas import tpu as pltpu
from jax.sharding import PartitionSpec as P

HEADS = 16
CORES = 2
F32 = jnp.float32
BF16 = jnp.bfloat16


def struct(shape, dtype):
    return jax.ShapeDtypeStruct(shape, dtype)


def call(body, out, *args, scratch=(), space=pltpu.VMEM):
    return pl.pallas_call(
        body,
        out_shape=out,
        in_specs=[pl.BlockSpec(memory_space=space)] * len(args),
        scratch_shapes=scratch,
        compiler_params=pltpu.CompilerParams(vmem_limit_bytes=24 * 2**20),
    )(*args)


def nt(left, right):
    return lax.dot_general(left, right, (((1,), (1,)), ((), ())), preferred_element_type=F32)


def nn(left, right):
    return jnp.dot(left, right, preferred_element_type=F32)


def unit_rows(values):
    inverse = lax.rsqrt(jnp.sum(values * values, axis=1, keepdims=True) + 1e-06)
    return values * inverse, inverse


def chain_back(grad_unit, unit_f, inverse):
    inner = jnp.sum(unit_f * grad_unit, axis=1, keepdims=True)
    return (grad_unit - unit_f * inner) * inverse


def slopes_of(left, right):
    logits = 10.0 * nt(left, right) - 2.0
    row = lax.broadcasted_iota(jnp.int32, logits.shape, 0)
    column = lax.broadcasted_iota(jnp.int32, logits.shape, 1)
    target = jnp.where(row == column, 1.0, 0.0)
    return (jax.nn.sigmoid(logits) - target).astype(BF16)


def split_terms(values):
    high = values.astype(BF16)
    rest = values - high.astype(F32)
    middle = rest.astype(BF16)
    return high, middle, (rest - middle.astype(F32)).astype(BF16)


def chip_and_core():
    place = lax.axis_index("grp")
    return place // CORES, lax.rem(place, CORES)


def prepare_kernel(
    probe_hbm, w_key_hbm, w_value_hbm, keys_ref, table_ref, blocks_ref, probe, w_key, w_value, sems
):
    part, width = w_key.shape
    chips, rows, _ = blocks_ref.shape
    copies = [
        pltpu.make_async_copy(source, target, sems.at[i])
        for i, (source, target) in enumerate(
            [(probe_hbm, probe), (w_key_hbm, w_key), (w_value_hbm, w_value)]
        )
    ]
    for copy in copies:
        copy.start()
    head = lax.broadcasted_iota(jnp.int32, (HEADS, width), 0)
    first = lax.broadcasted_iota(jnp.int32, (HEADS, width), 1) - head * (width // HEADS)
    inside = (first >= 0) & (first < width // HEADS)
    copies[0].wait()
    table = jnp.where(inside, probe[...].astype(F32).reshape(1, width), 0.0).astype(BF16)
    table_ref[...] = table
    copies[1].wait()
    keys_ref[...] = nt(table, w_key[...])
    copies[2].wait()
    wide = width // chips
    for q in range(chips):
        columns = w_value[:, q * wide : (q + 1) * wide]
        pieces = [columns[j * rows : (j + 1) * rows] for j in range(part // rows)]
        blocks_ref[q] = jnp.concatenate(pieces, axis=1)


def keys_kernel(keys_ref, table_ref, blocks_ref, other_ref, *out_refs):
    _, rows, packed = blocks_ref.shape
    chip, core = chip_and_core()
    own, other = keys_ref[...], nt(table_ref[...], other_ref[...])
    keys = [jnp.where(core == 0, own, other), jnp.where(core == 0, other, own)]
    keys = [
        term[h * rows : (h + 1) * rows]
        for term in split_terms(jnp.concatenate(keys, axis=1))
        for h in range(HEADS // rows)
    ]
    keys = jnp.concatenate(keys, axis=1)
    for m, out_ref in enumerate(out_refs):
        out_ref[:, :packed] = blocks_ref[chip ^ m]
        out_ref[:, packed:] = keys


def shard_kernel(chips, *refs):
    w_out_ref, out_ref = refs[chips:]
    _, rows, length = out_ref.shape
    part, width = w_out_ref.shape
    for m in range(chips):
        out_ref[m] = refs[m][:, :length]
    fit = length // width
    for j in range(part // rows):
        first = j % fit * width
        out_ref[chips + j // fit, :, first : first + width] = w_out_ref[j * rows : (j + 1) * rows]


def turn_kernel(x_ref, out_ref):
    out_ref[...] = x_ref[...].T


def attend_kernel(images, scaling, chips, x_ref, turned_ref, *refs):
    parts, outs, (placed, table, every) = refs[:chips], refs[chips:-3], refs[-3:]
    x = x_ref[...]
    width = x.shape[1]
    patches = x.shape[0] // images
    rows, length = parts[0].shape
    wide = width // chips
    pieces = table.shape[0] // rows
    chip, _ = chip_and_core()
    for m in range(chips):
        placed[chip ^ m] = parts[m][:, length - pieces * wide :]
    for j in range(pieces):
        for q in range(chips):
            table[j * rows : (j + 1) * rows, q * wide : (q + 1) * wide] = placed[
                q, :, j * wide : (j + 1) * wide
            ]
    parts = nn(table[...], turned_ref[...])
    scores = (parts[:HEADS] + parts[HEADS : 2 * HEADS] + parts[2 * HEADS :]) * scaling
    image = lax.broadcasted_iota(jnp.int32, (images, x.shape[0]), 0)
    first = lax.broadcasted_iota(jnp.int32, (images, x.shape[0]), 1) - image * patches
    own = (first >= 0) & (first < patches)
    spread = jnp.where(own[None], scores[:, None, :], -jnp.inf)
    expo = jnp.exp(spread - jnp.max(spread, axis=2, keepdims=True))
    weights = expo / jnp.sum(expo, axis=2, keepdims=True)
    weights = weights.reshape(HEADS * images, x.shape[0])
    every[...] = nn(weights.astype(BF16), x).astype(BF16).reshape(every.shape)
    for m, out_ref in enumerate(outs):
        out_ref[...] = every[chip ^ m]


def unpack_kernel(chips, *refs):
    w_out_ref, other_ref, w_value_ref, outs_ref = refs[chips:]
    part, width = w_out_ref.shape
    rows = other_ref.shape[1]
    chip, core = chip_and_core()
    for m in range(chips):
        for c, source in enumerate((refs[m], other_ref.at[m])):
            place = core if (c == 0) == (m == 0) else 1 - core
            for t in range(CORES):
                for j in range(part // rows):
                    first = (j * CORES + t) * part
                    w_value_ref[t, chip ^ m, place, j * rows : (j + 1) * rows] = source[
                        :, first : first + part
                    ]
    outs_ref[core] = w_out_ref[...]
    fit = other_ref.shape[2] // width
    for j in range(part // rows):
        first = j % fit * width
        outs_ref[1 - core, j * rows : (j + 1) * rows] = other_ref[
            chips + j // fit, :, first : first + width
        ]


def project_kernel(images, chips, *refs):
    mixed_refs, (w_value_ref, outs_ref), out_refs = refs[:chips], refs[chips : chips + 2], refs[chips + 2 :]
    _, rows, width = mixed_refs[0].shape
    part = outs_ref.shape[1]
    heads = rows // images
    head = lax.broadcasted_iota(jnp.int32, (chips, images, part), 2)
    embed = jnp.zeros((chips * images, width), F32)
    for t in range(CORES):
        mixed = jnp.concatenate([ref[t] for ref in mixed_refs], axis=0)
        every = nn(mixed, w_value_ref[t].reshape(width, part))
        every = every.reshape(chips, heads, images, part)
        pooled = every[:, 0]
        for h in range(1, heads):
            pooled = jnp.where(head >= h * (part // heads), every[:, h], pooled)
        pooled = pooled.reshape(chips * images, part).astype(BF16)
        embed = embed + nn(pooled, outs_ref[t])
    for m, out_ref in enumerate(out_refs):
        out_ref[...] = embed[m * images : (m + 1) * images].astype(BF16)


def unit_text_kernel(blocks, *refs):
    words_ref, unit_ref, inverse_ref = refs[blocks:]
    images = unit_ref.shape[0]
    texts = jnp.concatenate([ref[...].astype(F32) for ref in refs[:blocks]], axis=0)
    units, inverses = unit_rows(texts)
    words_ref[...] = units.astype(BF16)
    unit_ref[...] = units[:images]
    inverse_ref[...] = jnp.broadcast_to(inverses[:images], inverse_ref.shape)


def unit_image_kernel(chips, *refs):
    unit_ref, inverse_ref, rounded_ref = refs[chips + 1 :]
    embed = refs[0][...].astype(F32)
    for ref in refs[1:chips]:
        embed = embed + ref[...].astype(F32)
    unit, inverse = unit_rows(embed)
    unit_ref[...] = unit
    inverse_ref[...] = jnp.broadcast_to(inverse, inverse_ref.shape)
    rounded_ref[...] = unit.astype(BF16)


def grad_kernel(unit_ref, inverse_ref, *refs):
    others = [ref[...].astype(F32) for ref in refs[:-1]]
    others = jnp.concatenate(others, axis=0).astype(BF16)
    unit = unit_ref[...]
    slopes = slopes_of(unit.astype(BF16), others)
    refs[-1][...] = chain_back(10.0 * nn(slopes, others), unit, inverse_ref[:, :1])


def exchange(array, devices, flip, axis="grp"):
    return lax.ppermute(array, axis, [(i, i ^ flip) for i in range(devices)])


def all_blocks(array, blocks):
    return [array] + [
        lax.ppermute(array, "blk", [(i, (i + by) % blocks) for i in range(blocks)])
        for by in range(1, blocks)
    ]


def exchange_chips(arrays, devices):
    return [arrays[0]] + [
        exchange(array, devices, m * CORES + 1) for m, array in enumerate(arrays) if m
    ]


def local(patches, probe, w_key, w_value, w_out, texts):
    images, patch_count, width = patches.shape
    devices = lax.axis_size("grp")
    blocks = lax.axis_size("blk")
    part = w_key.shape[0]
    heads = HEADS // devices
    scaling = 1.0 / math.sqrt(width // HEADS)
    flat = patches.reshape(images * patch_count, width)

    rows = heads * images
    chips = devices // CORES
    wide = CORES * part
    packed = part // rows * wide
    fit = packed // width

    keys, table, columns = call(
        prepare_kernel,
        (
            struct((HEADS, part), F32),
            struct((HEADS, width), BF16),
            struct((chips, rows, packed), BF16),
        ),
        *[pltpu.with_memory_space_constraint(a, pltpu.HBM) for a in (probe, w_key, w_value)],
        scratch=[
            pltpu.VMEM(probe.shape, BF16),
            pltpu.VMEM(w_key.shape, BF16),
            pltpu.VMEM(w_value.shape, BF16),
            pltpu.SemaphoreType.DMA((3,)),
        ],
        space=pltpu.HBM,
    )
    parts = call(
        keys_kernel,
        [struct((rows, packed + 3 * HEADS // rows * wide), BF16)] * chips,
        keys,
        table,
        columns,
        exchange(w_key, devices, 1),
    )
    parts = exchange_chips(parts, devices)
    mixed = call(
        functools.partial(attend_kernel, images, scaling, chips),
        [struct((CORES, rows, width), BF16)] * chips,
        flat,
        call(turn_kernel, struct(flat.shape[::-1], BF16), flat),
        *parts,
        scratch=[
            pltpu.VMEM((chips, rows, 3 * HEADS // rows * wide), BF16),
            pltpu.VMEM((3 * HEADS, width), BF16),
            pltpu.VMEM((chips, CORES, rows, width), BF16),
        ],
    )
    shard = call(
        functools.partial(shard_kernel, chips),
        struct((chips + pl.cdiv(part // rows, fit), rows, packed), BF16),
        *parts,
        w_out,
    )
    w_values, w_outs = call(
        functools.partial(unpack_kernel, chips),
        (
            struct((CORES, chips, CORES, part, part), BF16),
            struct((CORES, part, width), BF16),
        ),
        *parts,
        w_out,
        exchange(shard, devices, 1),
    )
    partial_embed = call(
        functools.partial(project_kernel, images, chips),
        [struct((images, width), BF16)] * chips,
        *exchange_chips(mixed, devices),
        w_values,
        w_outs,
    )
    row, column = struct((images, width), F32), struct((images, 128), F32)
    words, unit_text, inverse_text = call(
        functools.partial(unit_text_kernel, blocks),
        (struct((blocks * images, width), BF16), row, column),
        *all_blocks(texts, blocks),
    )
    unit, inverse, rounded = call(
        functools.partial(unit_image_kernel, chips),
        (row, column, struct((images, width), BF16)),
        *exchange_chips(partial_embed, devices),
        inverse_text,
    )
    all_images = [exchange(rounded, blocks, m, "blk") for m in range(blocks - 1, 0, -1)]
    grad_image = call(grad_kernel, row, unit, inverse, words)
    grad_text = call(grad_kernel, row, unit_text, inverse_text, rounded, *all_images)
    return grad_image, grad_text


def solution(mesh):
    in_specs = (
        P(("grp", "blk"), None, None),
        P(),
        P("grp", None),
        P("grp", None),
        P("grp", None),
        P(("grp", "blk"), None),
    )
    out_specs = (P(("grp", "blk"), None), P(("grp", "blk"), None))
    return jax.shard_map(local, mesh=mesh, in_specs=in_specs, out_specs=out_specs, check_vma=False)
```

```python
import functools
import math

import jax
import jax.numpy as jnp
from jax import lax
from jax.experimental import pallas as pl
from jax.experimental.pallas import tpu as pltpu
from jax.sharding import PartitionSpec as P

HEADS = 16
CORES = 2
F32 = jnp.float32
BF16 = jnp.bfloat16


def struct(shape, dtype):
    return jax.ShapeDtypeStruct(shape, dtype)


def call(body, out, *args, scratch=(), space=pltpu.VMEM, cost=None):
    return pl.pallas_call(
        body,
        out_shape=out,
        in_specs=[pl.BlockSpec(memory_space=space)] * len(args),
        scratch_shapes=scratch,
        cost_estimate=cost and pl.CostEstimate(flops=cost, bytes_accessed=0, transcendentals=0),
        compiler_params=pltpu.CompilerParams(vmem_limit_bytes=24 * 2**20),
    )(*args)


def nt(left, right):
    return lax.dot_general(left, right, (((1,), (1,)), ((), ())), preferred_element_type=F32)


def nn(left, right):
    return jnp.dot(left, right, preferred_element_type=F32)


def unit_rows(values):
    inverse = lax.rsqrt(jnp.sum(values * values, axis=1, keepdims=True) + 1e-06)
    return values * inverse, inverse


def chain_back(grad_unit, unit_f, inverse):
    inner = jnp.sum(unit_f * grad_unit, axis=1, keepdims=True)
    return (grad_unit - unit_f * inner) * inverse


def slopes_of(left, right):
    logits = 10.0 * nt(left, right) - 2.0
    row = lax.broadcasted_iota(jnp.int32, logits.shape, 0)
    column = lax.broadcasted_iota(jnp.int32, logits.shape, 1)
    target = jnp.where(row == column, 1.0, 0.0)
    return (jax.nn.sigmoid(logits) - target).astype(BF16)


def split_terms(values):
    high = values.astype(BF16)
    rest = values - high.astype(F32)
    middle = rest.astype(BF16)
    return high, middle, (rest - middle.astype(F32)).astype(BF16)


def chip_and_core():
    place = lax.axis_index("grp")
    return place // CORES, lax.rem(place, CORES)


def prepare_kernel(chips, probe_hbm, w_key_hbm, w_value_hbm, *refs):
    out_refs, (probe, w_key, w_value, blocks, sems) = refs[:chips], refs[chips:]
    part, width = w_key.shape
    _, rows, packed = blocks.shape
    copies = [
        pltpu.make_async_copy(source, target, sems.at[i])
        for i, (source, target) in enumerate(
            [(probe_hbm, probe), (w_key_hbm, w_key), (w_value_hbm, w_value)]
        )
    ]
    for copy in copies:
        copy.start()
    head = lax.broadcasted_iota(jnp.int32, (HEADS, width), 0)
    first = lax.broadcasted_iota(jnp.int32, (HEADS, width), 1) - head * (width // HEADS)
    inside = (first >= 0) & (first < width // HEADS)
    copies[0].wait()
    table = jnp.where(inside, probe[...].astype(F32).reshape(1, width), 0.0).astype(BF16)
    copies[1].wait()
    keys = [
        term[h * rows : (h + 1) * rows]
        for term in split_terms(nt(table, w_key[...]))
        for h in range(HEADS // rows)
    ]
    keys = jnp.concatenate(keys, axis=1)
    copies[2].wait()
    wide = width // chips
    for q in range(chips):
        columns = w_value[:, q * wide : (q + 1) * wide]
        pieces = [columns[j * rows : (j + 1) * rows] for j in range(part // rows)]
        blocks[q] = jnp.concatenate(pieces, axis=1)
    chip, _ = chip_and_core()
    for m, out_ref in enumerate(out_refs):
        out_ref[:, :packed] = blocks[chip ^ m]
        out_ref[:, packed:] = keys


def pack_keys_kernel(chips, *refs):
    length = refs[-1].shape[2]
    for m in range(chips):
        refs[-1][m] = refs[m][:, refs[m].shape[1] - length :]


def turn_kernel(x_ref, _, out_ref):
    out_ref[...] = x_ref[...].T


def shard_kernel(chips, *refs):
    w_out_ref, _, out_ref = refs[chips:]
    _, rows, length = out_ref.shape
    part, width = w_out_ref.shape
    for m in range(chips):
        out_ref[m] = refs[m][:, :length]
    fit = length // width
    for j in range(part // rows):
        first = j % fit * width
        out_ref[chips + j // fit, :, first : first + width] = w_out_ref[j * rows : (j + 1) * rows]


def attend_kernel(images, scaling, chips, x_ref, own_ref, other_ref, *refs):
    outs, (placed, table, every) = refs[:chips], refs[chips:]
    x = x_ref[...]
    width = x.shape[1]
    patches = x.shape[0] // images
    _, rows, length = own_ref.shape
    part = width // (chips * CORES)
    chip, core = chip_and_core()
    for m in range(chips):
        place = core if m == 0 else 1 - core
        placed[chip ^ m, place] = own_ref[m]
        placed[chip ^ m, 1 - place] = other_ref[m]
    for j in range(length // part):
        for k in range(chips * CORES):
            table[j * rows : (j + 1) * rows, k * part : (k + 1) * part] = placed[
                k // CORES, k % CORES, :, j * part : (j + 1) * part
            ]
    parts = nt(table[...], x)
    scores = (parts[:HEADS] + parts[HEADS : 2 * HEADS] + parts[2 * HEADS :]) * scaling
    image = lax.broadcasted_iota(jnp.int32, (images, x.shape[0]), 0)
    first = lax.broadcasted_iota(jnp.int32, (images, x.shape[0]), 1) - image * patches
    own = (first >= 0) & (first < patches)
    spread = jnp.where(own[None], scores[:, None, :], -jnp.inf)
    expo = jnp.exp(spread - jnp.max(spread, axis=2, keepdims=True))
    weights = expo / jnp.sum(expo, axis=2, keepdims=True)
    weights = weights.reshape(HEADS * images, x.shape[0])
    every[...] = nn(weights.astype(BF16), x).astype(BF16).reshape(every.shape)
    for m, out_ref in enumerate(outs):
        out_ref[...] = every[chip ^ m]


def unpack_kernel(chips, *refs):
    w_out_ref, other_ref, w_value_ref, outs_ref = refs[chips:]
    part, width = w_out_ref.shape
    rows = other_ref.shape[1]
    chip, core = chip_and_core()
    for m in range(chips):
        for c, source in enumerate((refs[m], other_ref.at[m])):
            place = core if (c == 0) == (m == 0) else 1 - core
            for t in range(CORES):
                for j in range(part // rows):
                    first = (j * CORES + t) * part
                    w_value_ref[t, chip ^ m, place, j * rows : (j + 1) * rows] = source[
                        :, first : first + part
                    ]
    outs_ref[core] = w_out_ref[...]
    fit = other_ref.shape[2] // width
    for j in range(part // rows):
        first = j % fit * width
        outs_ref[1 - core, j * rows : (j + 1) * rows] = other_ref[
            chips + j // fit, :, first : first + width
        ]


def project_kernel(images, chips, *refs):
    mixed_refs, (w_value_ref, outs_ref), out_refs = refs[:chips], refs[chips : chips + 2], refs[chips + 2 :]
    _, rows, width = mixed_refs[0].shape
    part = outs_ref.shape[1]
    heads = rows // images
    head = lax.broadcasted_iota(jnp.int32, (chips, images, part), 2)
    embed = jnp.zeros((chips * images, width), F32)
    for t in range(CORES):
        mixed = jnp.concatenate([ref[t] for ref in mixed_refs], axis=0)
        every = nn(mixed, w_value_ref[t].reshape(width, part))
        every = every.reshape(chips, heads, images, part)
        pooled = every[:, 0]
        for h in range(1, heads):
            pooled = jnp.where(head >= h * (part // heads), every[:, h], pooled)
        pooled = pooled.reshape(chips * images, part).astype(BF16)
        embed = embed + nn(pooled, outs_ref[t])
    for m, out_ref in enumerate(out_refs):
        out_ref[...] = embed[m * images : (m + 1) * images].astype(BF16)


def unit_text_kernel(blocks, *refs):
    words_ref, unit_ref, inverse_ref = refs[blocks:]
    images = unit_ref.shape[0]
    texts = jnp.concatenate([ref[...].astype(F32) for ref in refs[:blocks]], axis=0)
    units, inverses = unit_rows(texts)
    words_ref[...] = units.astype(BF16)
    unit_ref[...] = units[:images]
    inverse_ref[...] = jnp.broadcast_to(inverses[:images], inverse_ref.shape)


def unit_image_kernel(chips, *refs):
    unit_ref, inverse_ref, rounded_ref = refs[chips + 1 :]
    embed = refs[0][...].astype(F32)
    for ref in refs[1:chips]:
        embed = embed + ref[...].astype(F32)
    unit, inverse = unit_rows(embed)
    unit_ref[...] = unit
    inverse_ref[...] = jnp.broadcast_to(inverse, inverse_ref.shape)
    rounded_ref[...] = unit.astype(BF16)


def grad_kernel(unit_ref, inverse_ref, *refs):
    others = [ref[...].astype(F32) for ref in refs[:-1]]
    others = jnp.concatenate(others, axis=0).astype(BF16)
    unit = unit_ref[...]
    slopes = slopes_of(unit.astype(BF16), others)
    refs[-1][...] = chain_back(10.0 * nn(slopes, others), unit, inverse_ref[:, :1])


def exchange(array, devices, flip, axis="grp"):
    return lax.ppermute(array, axis, [(i, i ^ flip) for i in range(devices)])


def all_blocks(array, blocks):
    return [array] + [
        lax.ppermute(array, "blk", [(i, (i + by) % blocks) for i in range(blocks)])
        for by in range(1, blocks)
    ]


def exchange_chips(arrays, devices):
    return [arrays[0]] + [
        exchange(array, devices, m * CORES + 1) for m, array in enumerate(arrays) if m
    ]


def local(patches, probe, w_key, w_value, w_out, texts):
    images, patch_count, width = patches.shape
    devices = lax.axis_size("grp")
    blocks = lax.axis_size("blk")
    part = w_key.shape[0]
    heads = HEADS // devices
    scaling = 1.0 / math.sqrt(width // HEADS)
    flat = patches.reshape(images * patch_count, width)

    rows = heads * images
    chips = devices // CORES
    wide = CORES * part
    packed = part // rows * wide
    fit = packed // width

    length = 3 * HEADS // rows * part
    parts = call(
        functools.partial(prepare_kernel, chips),
        [struct((rows, packed + length), BF16)] * chips,
        *[pltpu.with_memory_space_constraint(a, pltpu.HBM) for a in (probe, w_key, w_value)],
        scratch=[
            pltpu.VMEM(probe.shape, BF16),
            pltpu.VMEM(w_key.shape, BF16),
            pltpu.VMEM(w_value.shape, BF16),
            pltpu.VMEM((chips, rows, packed), BF16),
            pltpu.SemaphoreType.DMA((3,)),
        ],
        space=pltpu.HBM,
    )
    parts = exchange_chips(parts, devices)
    keys = call(
        functools.partial(pack_keys_kernel, chips), struct((chips, rows, length), BF16), *parts
    )
    shard = call(
        functools.partial(shard_kernel, chips),
        struct((chips + pl.cdiv(part // rows, fit), rows, packed), BF16),
        *parts,
        w_out,
        keys,
    )
    mixed = call(
        functools.partial(attend_kernel, images, scaling, chips),
        [struct((CORES, rows, width), BF16)] * chips,
        flat,
        keys,
        exchange(keys, devices, 1),
        cost=10000000000,
        scratch=[
            pltpu.VMEM((chips, CORES, rows, length), BF16),
            pltpu.VMEM((3 * HEADS, width), BF16),
            pltpu.VMEM((chips, CORES, rows, width), BF16),
        ],
    )
    w_values, w_outs = call(
        functools.partial(unpack_kernel, chips),
        (
            struct((CORES, chips, CORES, part, part), BF16),
            struct((CORES, part, width), BF16),
        ),
        *parts,
        w_out,
        exchange(shard, devices, 1),
    )
    partial_embed = call(
        functools.partial(project_kernel, images, chips),
        [struct((images, width), BF16)] * chips,
        *exchange_chips(mixed, devices),
        w_values,
        w_outs,
    )
    row, column = struct((images, width), F32), struct((images, 128), F32)
    words, unit_text, inverse_text = call(
        functools.partial(unit_text_kernel, blocks),
        (struct((blocks * images, width), BF16), row, column),
        *all_blocks(texts, blocks),
    )
    unit, inverse, rounded = call(
        functools.partial(unit_image_kernel, chips),
        (row, column, struct((images, width), BF16)),
        *exchange_chips(partial_embed, devices),
        inverse_text,
    )
    all_images = [exchange(rounded, blocks, m, "blk") for m in range(blocks - 1, 0, -1)]
    grad_image = call(grad_kernel, row, unit, inverse, words)
    grad_text = call(grad_kernel, row, unit_text, inverse_text, rounded, *all_images)
    return grad_image, grad_text


def solution(mesh):
    in_specs = (
        P(("grp", "blk"), None, None),
        P(),
        P("grp", None),
        P("grp", None),
        P("grp", None),
        P(("grp", "blk"), None),
    )
    out_specs = (P(("grp", "blk"), None), P(("grp", "blk"), None))
    return jax.shard_map(local, mesh=mesh, in_specs=in_specs, out_specs=out_specs, check_vma=False)
```

```python
import functools
import math

import jax
import jax.numpy as jnp
from jax import lax
from jax.experimental import pallas as pl
from jax.experimental.pallas import tpu as pltpu
from jax.sharding import PartitionSpec as P

HEADS = 16
CORES = 2
F32 = jnp.float32
BF16 = jnp.bfloat16


def struct(shape, dtype):
    return jax.ShapeDtypeStruct(shape, dtype)


def call(body, out, *args, scratch=(), space=pltpu.VMEM, cost=None):
    return pl.pallas_call(
        body,
        out_shape=out,
        in_specs=[pl.BlockSpec(memory_space=space)] * len(args),
        scratch_shapes=scratch,
        cost_estimate=cost and pl.CostEstimate(flops=cost, bytes_accessed=0, transcendentals=0),
        compiler_params=pltpu.CompilerParams(vmem_limit_bytes=24 * 2**20),
    )(*args)


def nt(left, right):
    return lax.dot_general(left, right, (((1,), (1,)), ((), ())), preferred_element_type=F32)


def nn(left, right):
    return jnp.dot(left, right, preferred_element_type=F32)


def unit_rows(values):
    inverse = lax.rsqrt(jnp.sum(values * values, axis=1, keepdims=True) + 1e-06)
    return values * inverse, inverse


def chain_back(grad_unit, unit_f, inverse):
    inner = jnp.sum(unit_f * grad_unit, axis=1, keepdims=True)
    return (grad_unit - unit_f * inner) * inverse


def slopes_of(left, right):
    logits = 10.0 * nt(left, right) - 2.0
    row = lax.broadcasted_iota(jnp.int32, logits.shape, 0)
    column = lax.broadcasted_iota(jnp.int32, logits.shape, 1)
    target = jnp.where(row == column, 1.0, 0.0)
    return (jax.nn.sigmoid(logits) - target).astype(BF16)


def split_terms(values):
    high = values.astype(BF16)
    rest = values - high.astype(F32)
    middle = rest.astype(BF16)
    return high, middle, (rest - middle.astype(F32)).astype(BF16)


def flips(chips):
    return [0, *range(chips - 1, chips - 2, -1), *range(1, chips - 1)]


def chip_and_core():
    place = lax.axis_index("grp")
    return place // CORES, lax.rem(place, CORES)


def prepare_kernel(chips, probe_hbm, w_key_hbm, w_value_hbm, *refs):
    out_refs, (probe, w_key, w_value, blocks, sems) = refs[:chips], refs[chips:]
    part, width = w_key.shape
    _, rows, packed = blocks.shape
    copies = [
        pltpu.make_async_copy(source, target, sems.at[i])
        for i, (source, target) in enumerate(
            [(probe_hbm, probe), (w_key_hbm, w_key), (w_value_hbm, w_value)]
        )
    ]
    for copy in copies:
        copy.start()
    head = lax.broadcasted_iota(jnp.int32, (HEADS, width), 0)
    first = lax.broadcasted_iota(jnp.int32, (HEADS, width), 1) - head * (width // HEADS)
    inside = (first >= 0) & (first < width // HEADS)
    copies[0].wait()
    table = jnp.where(inside, probe[...].astype(F32).reshape(1, width), 0.0).astype(BF16)
    copies[1].wait()
    keys = [
        term[h * rows : (h + 1) * rows]
        for term in split_terms(nt(table, w_key[...]))
        for h in range(HEADS // rows)
    ]
    keys = jnp.concatenate(keys, axis=1)
    copies[2].wait()
    wide = width // chips
    for q in range(chips):
        columns = w_value[:, q * wide : (q + 1) * wide]
        pieces = [columns[j * rows : (j + 1) * rows] for j in range(part // rows)]
        blocks[q] = jnp.concatenate(pieces, axis=1)
    chip, _ = chip_and_core()
    for m, out_ref in zip(flips(chips), out_refs):
        out_ref[:, :packed] = blocks[chip ^ m]
        out_ref[:, packed:] = keys


def pack_keys_kernel(chips, *refs):
    length = refs[-1].shape[2]
    for m in range(chips):
        refs[-1][m] = refs[m][:, refs[m].shape[1] - length :]


def turn_kernel(x_ref, _, out_ref):
    out_ref[...] = x_ref[...].T


def shard_kernel(chips, *refs):
    w_out_ref, _, out_ref = refs[chips:]
    _, rows, length = out_ref.shape
    part, width = w_out_ref.shape
    for m in range(chips):
        out_ref[m] = refs[m][:, :length]
    fit = length // width
    for j in range(part // rows):
        first = j % fit * width
        out_ref[chips + j // fit, :, first : first + width] = w_out_ref[j * rows : (j + 1) * rows]


def attend_kernel(images, scaling, chips, x_ref, own_ref, other_ref, *refs):
    outs, (placed, table, every) = refs[:chips], refs[chips:]
    x = x_ref[...]
    width = x.shape[1]
    patches = x.shape[0] // images
    _, rows, length = own_ref.shape
    part = width // (chips * CORES)
    chip, core = chip_and_core()
    for i, m in enumerate(flips(chips)):
        place = core if m == 0 else 1 - core
        placed[chip ^ m, place] = own_ref[i]
        placed[chip ^ m, 1 - place] = other_ref[i]
    for j in range(length // part):
        for k in range(chips * CORES):
            table[j * rows : (j + 1) * rows, k * part : (k + 1) * part] = placed[
                k // CORES, k % CORES, :, j * part : (j + 1) * part
            ]
    parts = nt(table[...], x)
    scores = (parts[:HEADS] + parts[HEADS : 2 * HEADS] + parts[2 * HEADS :]) * scaling
    image = lax.broadcasted_iota(jnp.int32, (images, x.shape[0]), 0)
    first = lax.broadcasted_iota(jnp.int32, (images, x.shape[0]), 1) - image * patches
    own = (first >= 0) & (first < patches)
    spread = jnp.where(own[None], scores[:, None, :], -jnp.inf)
    expo = jnp.exp(spread - jnp.max(spread, axis=2, keepdims=True))
    weights = expo / jnp.sum(expo, axis=2, keepdims=True)
    weights = weights.reshape(HEADS * images, x.shape[0])
    every[...] = nn(weights.astype(BF16), x).astype(BF16).reshape(every.shape)
    for m, out_ref in zip(flips(chips), outs):
        out_ref[...] = every[chip ^ m]


def unpack_kernel(chips, *refs):
    w_out_ref, other_ref, w_value_ref, outs_ref = refs[chips:]
    part, width = w_out_ref.shape
    rows = other_ref.shape[1]
    chip, core = chip_and_core()
    for i, m in enumerate(flips(chips)):
        for c, source in enumerate((refs[i], other_ref.at[i])):
            place = core if (c == 0) == (m == 0) else 1 - core
            for t in range(CORES):
                for j in range(part // rows):
                    first = (j * CORES + t) * part
                    w_value_ref[t, chip ^ m, place, j * rows : (j + 1) * rows] = source[
                        :, first : first + part
                    ]
    outs_ref[core] = w_out_ref[...]
    fit = other_ref.shape[2] // width
    for j in range(part // rows):
        first = j % fit * width
        outs_ref[1 - core, j * rows : (j + 1) * rows] = other_ref[
            chips + j // fit, :, first : first + width
        ]


def project_kernel(images, chips, *refs):
    mixed_refs, (w_value_ref, outs_ref), out_refs = refs[:chips], refs[chips : chips + 2], refs[chips + 2 :]
    _, rows, width = mixed_refs[0].shape
    part = outs_ref.shape[1]
    heads = rows // images
    head = lax.broadcasted_iota(jnp.int32, (chips, images, part), 2)
    embed = jnp.zeros((chips * images, width), F32)
    for t in range(CORES):
        mixed = jnp.concatenate([ref[t] for ref in mixed_refs], axis=0)
        every = nn(mixed, w_value_ref[t].reshape(width, part))
        every = every.reshape(chips, heads, images, part)
        pooled = every[:, 0]
        for h in range(1, heads):
            pooled = jnp.where(head >= h * (part // heads), every[:, h], pooled)
        pooled = pooled.reshape(chips * images, part).astype(BF16)
        embed = embed + nn(pooled, outs_ref[t])
    for m, out_ref in enumerate(out_refs):
        out_ref[...] = embed[m * images : (m + 1) * images].astype(BF16)


def unit_text_kernel(blocks, *refs):
    words_ref, unit_ref, inverse_ref = refs[blocks:]
    images = unit_ref.shape[0]
    texts = jnp.concatenate([ref[...].astype(F32) for ref in refs[:blocks]], axis=0)
    units, inverses = unit_rows(texts)
    words_ref[...] = units.astype(BF16)
    unit_ref[...] = units[:images]
    inverse_ref[...] = jnp.broadcast_to(inverses[:images], inverse_ref.shape)


def unit_image_kernel(chips, *refs):
    unit_ref, inverse_ref, rounded_ref = refs[chips + 1 :]
    embed = refs[0][...].astype(F32)
    for ref in refs[1:chips]:
        embed = embed + ref[...].astype(F32)
    unit, inverse = unit_rows(embed)
    unit_ref[...] = unit
    inverse_ref[...] = jnp.broadcast_to(inverse, inverse_ref.shape)
    rounded_ref[...] = unit.astype(BF16)


def grad_kernel(unit_ref, inverse_ref, *refs):
    others = [ref[...].astype(F32) for ref in refs[:-1]]
    others = jnp.concatenate(others, axis=0).astype(BF16)
    unit = unit_ref[...]
    slopes = slopes_of(unit.astype(BF16), others)
    refs[-1][...] = chain_back(10.0 * nn(slopes, others), unit, inverse_ref[:, :1])


def exchange(array, devices, flip, axis="grp"):
    return lax.ppermute(array, axis, [(i, i ^ flip) for i in range(devices)])


def all_blocks(array, blocks):
    return [array] + [
        lax.ppermute(array, "blk", [(i, (i + by) % blocks) for i in range(blocks)])
        for by in range(1, blocks)
    ]


def exchange_chips(arrays, devices):
    return [
        exchange(array, devices, m * CORES + 1) if m else array
        for m, array in zip(flips(len(arrays)), arrays)
    ]


def local(patches, probe, w_key, w_value, w_out, texts):
    images, patch_count, width = patches.shape
    devices = lax.axis_size("grp")
    blocks = lax.axis_size("blk")
    part = w_key.shape[0]
    heads = HEADS // devices
    scaling = 1.0 / math.sqrt(width // HEADS)
    flat = patches.reshape(images * patch_count, width)

    rows = heads * images
    chips = devices // CORES
    wide = CORES * part
    packed = part // rows * wide
    fit = packed // width

    length = 3 * HEADS // rows * part
    parts = call(
        functools.partial(prepare_kernel, chips),
        [struct((rows, packed + length), BF16)] * chips,
        *[pltpu.with_memory_space_constraint(a, pltpu.HBM) for a in (probe, w_key, w_value)],
        scratch=[
            pltpu.VMEM(probe.shape, BF16),
            pltpu.VMEM(w_key.shape, BF16),
            pltpu.VMEM(w_value.shape, BF16),
            pltpu.VMEM((chips, rows, packed), BF16),
            pltpu.SemaphoreType.DMA((3,)),
        ],
        space=pltpu.HBM,
    )
    parts = exchange_chips(parts, devices)
    keys = call(
        functools.partial(pack_keys_kernel, chips), struct((chips, rows, length), BF16), *parts
    )
    shard = call(
        functools.partial(shard_kernel, chips),
        struct((chips + pl.cdiv(part // rows, fit), rows, packed), BF16),
        *parts,
        w_out,
        keys,
    )
    mixed = call(
        functools.partial(attend_kernel, images, scaling, chips),
        [struct((CORES, rows, width), BF16)] * chips,
        flat,
        keys,
        exchange(keys, devices, 1),
        cost=10000000000,
        scratch=[
            pltpu.VMEM((chips, CORES, rows, length), BF16),
            pltpu.VMEM((3 * HEADS, width), BF16),
            pltpu.VMEM((chips, CORES, rows, width), BF16),
        ],
    )
    w_values, w_outs = call(
        functools.partial(unpack_kernel, chips),
        (
            struct((CORES, chips, CORES, part, part), BF16),
            struct((CORES, part, width), BF16),
        ),
        *parts,
        w_out,
        exchange(shard, devices, 1),
    )
    partial_embed = call(
        functools.partial(project_kernel, images, chips),
        [struct((images, width), BF16)] * chips,
        *exchange_chips(mixed, devices),
        w_values,
        w_outs,
    )
    row, column = struct((images, width), F32), struct((images, 128), F32)
    words, unit_text, inverse_text = call(
        functools.partial(unit_text_kernel, blocks),
        (struct((blocks * images, width), BF16), row, column),
        *all_blocks(texts, blocks),
    )
    unit, inverse, rounded = call(
        functools.partial(unit_image_kernel, chips),
        (row, column, struct((images, width), BF16)),
        *exchange_chips(partial_embed, devices),
        inverse_text,
    )
    all_images = [exchange(rounded, blocks, m, "blk") for m in range(blocks - 1, 0, -1)]
    grad_image = call(grad_kernel, row, unit, inverse, words)
    grad_text = call(grad_kernel, row, unit_text, inverse_text, rounded, *all_images)
    return grad_image, grad_text


def solution(mesh):
    in_specs = (
        P(("grp", "blk"), None, None),
        P(),
        P("grp", None),
        P("grp", None),
        P("grp", None),
        P(("grp", "blk"), None),
    )
    out_specs = (P(("grp", "blk"), None), P(("grp", "blk"), None))
    return jax.shard_map(local, mesh=mesh, in_specs=in_specs, out_specs=out_specs, check_vma=False)
```

```python
import functools
import math

import jax
import jax.numpy as jnp
from jax import lax
from jax.experimental import pallas as pl
from jax.experimental.pallas import tpu as pltpu
from jax.sharding import PartitionSpec as P

HEADS = 16
CORES = 2
F32 = jnp.float32
BF16 = jnp.bfloat16


def struct(shape, dtype):
    return jax.ShapeDtypeStruct(shape, dtype)


def call(body, out, *args, scratch=(), space=pltpu.VMEM, cost=None):
    return pl.pallas_call(
        body,
        out_shape=out,
        in_specs=[pl.BlockSpec(memory_space=space)] * len(args),
        scratch_shapes=scratch,
        cost_estimate=cost and pl.CostEstimate(flops=cost, bytes_accessed=0, transcendentals=0),
        compiler_params=pltpu.CompilerParams(vmem_limit_bytes=24 * 2**20),
    )(*args)


def nt(left, right):
    return lax.dot_general(left, right, (((1,), (1,)), ((), ())), preferred_element_type=F32)


def nn(left, right):
    return jnp.dot(left, right, preferred_element_type=F32)


def unit_rows(values):
    inverse = lax.rsqrt(jnp.sum(values * values, axis=1, keepdims=True) + 1e-06)
    return values * inverse, inverse


def chain_back(grad_unit, unit_f, inverse):
    inner = jnp.sum(unit_f * grad_unit, axis=1, keepdims=True)
    return (grad_unit - unit_f * inner) * inverse


def slopes_of(left, right):
    logits = 10.0 * nt(left, right) - 2.0
    row = lax.broadcasted_iota(jnp.int32, logits.shape, 0)
    column = lax.broadcasted_iota(jnp.int32, logits.shape, 1)
    target = jnp.where(row == column, 1.0, 0.0)
    return (jax.nn.sigmoid(logits) - target).astype(BF16)


def split_terms(values):
    high = values.astype(BF16)
    rest = values - high.astype(F32)
    middle = rest.astype(BF16)
    return high, middle, (rest - middle.astype(F32)).astype(BF16)


def far_first(chips):
    return [0, chips - 1, *range(1, chips - 1)]


def chip_and_core():
    place = lax.axis_index("grp")
    return place // CORES, lax.rem(place, CORES)


def prepare_kernel(chips, probe_hbm, w_key_hbm, w_value_hbm, *refs):
    out_refs, (probe, w_key, w_value, blocks, sems) = refs[:chips], refs[chips:]
    part, width = w_key.shape
    _, rows, packed = blocks.shape
    copies = [
        pltpu.make_async_copy(source, target, sems.at[i])
        for i, (source, target) in enumerate(
            [(probe_hbm, probe), (w_key_hbm, w_key), (w_value_hbm, w_value)]
        )
    ]
    for copy in copies:
        copy.start()
    head = lax.broadcasted_iota(jnp.int32, (HEADS, width), 0)
    first = lax.broadcasted_iota(jnp.int32, (HEADS, width), 1) - head * (width // HEADS)
    inside = (first >= 0) & (first < width // HEADS)
    copies[0].wait()
    table = jnp.where(inside, probe[...].astype(F32).reshape(1, width), 0.0).astype(BF16)
    copies[1].wait()
    keys = [
        term[h * rows : (h + 1) * rows]
        for term in split_terms(nt(table, w_key[...]))
        for h in range(HEADS // rows)
    ]
    keys = jnp.concatenate(keys, axis=1)
    copies[2].wait()
    wide = width // chips
    for q in range(chips):
        columns = w_value[:, q * wide : (q + 1) * wide]
        pieces = [columns[j * rows : (j + 1) * rows] for j in range(part // rows)]
        blocks[q] = jnp.concatenate(pieces, axis=1)
    chip, _ = chip_and_core()
    for m, out_ref in enumerate(out_refs):
        out_ref[:, :packed] = blocks[chip ^ m]
        out_ref[:, packed:] = keys


def pack_keys_kernel(chips, *refs):
    length = refs[-1].shape[2]
    for m in range(chips):
        refs[-1][m] = refs[m][:, refs[m].shape[1] - length :]


def turn_kernel(x_ref, _, out_ref):
    out_ref[...] = x_ref[...].T


def shard_kernel(chips, *refs):
    w_out_ref, _, out_ref = refs[chips:]
    _, rows, length = out_ref.shape
    part, width = w_out_ref.shape
    for m in range(chips):
        out_ref[m] = refs[m][:, :length]
    fit = length // width
    for j in range(part // rows):
        first = j % fit * width
        out_ref[chips + j // fit, :, first : first + width] = w_out_ref[j * rows : (j + 1) * rows]


def attend_kernel(images, scaling, chips, x_ref, own_ref, other_ref, *refs):
    outs, (placed, table, every) = refs[:chips], refs[chips:]
    x = x_ref[...]
    width = x.shape[1]
    patches = x.shape[0] // images
    _, rows, length = own_ref.shape
    part = width // (chips * CORES)
    chip, core = chip_and_core()
    for m in range(chips):
        place = core if m == 0 else 1 - core
        placed[chip ^ m, place] = own_ref[m]
        placed[chip ^ m, 1 - place] = other_ref[m]
    for j in range(length // part):
        for k in range(chips * CORES):
            table[j * rows : (j + 1) * rows, k * part : (k + 1) * part] = placed[
                k // CORES, k % CORES, :, j * part : (j + 1) * part
            ]
    parts = nt(table[...], x)
    scores = (parts[:HEADS] + parts[HEADS : 2 * HEADS] + parts[2 * HEADS :]) * scaling
    image = lax.broadcasted_iota(jnp.int32, (images, x.shape[0]), 0)
    first = lax.broadcasted_iota(jnp.int32, (images, x.shape[0]), 1) - image * patches
    own = (first >= 0) & (first < patches)
    spread = jnp.where(own[None], scores[:, None, :], -jnp.inf)
    expo = jnp.exp(spread - jnp.max(spread, axis=2, keepdims=True))
    weights = expo / jnp.sum(expo, axis=2, keepdims=True)
    weights = weights.reshape(HEADS * images, x.shape[0])
    every[...] = nn(weights.astype(BF16), x).astype(BF16).reshape(every.shape)
    for m, out_ref in zip(far_first(chips), outs):
        out_ref[...] = every[chip ^ m]


def unpack_kernel(chips, *refs):
    w_out_ref, other_ref, w_value_ref, outs_ref = refs[chips:]
    part, width = w_out_ref.shape
    rows = other_ref.shape[1]
    chip, core = chip_and_core()
    for m in range(chips):
        for c, source in enumerate((refs[m], other_ref.at[m])):
            place = core if (c == 0) == (m == 0) else 1 - core
            for t in range(CORES):
                for j in range(part // rows):
                    first = (j * CORES + t) * part
                    w_value_ref[t, chip ^ m, place, j * rows : (j + 1) * rows] = source[
                        :, first : first + part
                    ]
    outs_ref[core] = w_out_ref[...]
    fit = other_ref.shape[2] // width
    for j in range(part // rows):
        first = j % fit * width
        outs_ref[1 - core, j * rows : (j + 1) * rows] = other_ref[
            chips + j // fit, :, first : first + width
        ]


def project_kernel(images, chips, *refs):
    mixed_refs, (w_value_ref, outs_ref), out_refs = refs[:chips], refs[chips : chips + 2], refs[chips + 2 :]
    _, rows, width = mixed_refs[0].shape
    part = outs_ref.shape[1]
    heads = rows // images
    head = lax.broadcasted_iota(jnp.int32, (chips, images, part), 2)
    embed = jnp.zeros((chips * images, width), F32)
    for t in range(CORES):
        mixed = jnp.concatenate([ref[t] for ref in mixed_refs], axis=0)
        every = nn(mixed, w_value_ref[t].reshape(width, part))
        every = every.reshape(chips, heads, images, part)
        pooled = every[:, 0]
        for h in range(1, heads):
            pooled = jnp.where(head >= h * (part // heads), every[:, h], pooled)
        pooled = pooled.reshape(chips * images, part).astype(BF16)
        embed = embed + nn(pooled, outs_ref[t])
    for m, out_ref in enumerate(out_refs):
        out_ref[...] = embed[m * images : (m + 1) * images].astype(BF16)


def unit_text_kernel(blocks, *refs):
    words_ref, unit_ref, inverse_ref = refs[blocks:]
    images = unit_ref.shape[0]
    texts = jnp.concatenate([ref[...].astype(F32) for ref in refs[:blocks]], axis=0)
    units, inverses = unit_rows(texts)
    words_ref[...] = units.astype(BF16)
    unit_ref[...] = units[:images]
    inverse_ref[...] = jnp.broadcast_to(inverses[:images], inverse_ref.shape)


def unit_image_kernel(chips, *refs):
    unit_ref, inverse_ref, rounded_ref = refs[chips + 1 :]
    embed = refs[0][...].astype(F32)
    for ref in refs[1:chips]:
        embed = embed + ref[...].astype(F32)
    unit, inverse = unit_rows(embed)
    unit_ref[...] = unit
    inverse_ref[...] = jnp.broadcast_to(inverse, inverse_ref.shape)
    rounded_ref[...] = unit.astype(BF16)


def grad_kernel(unit_ref, inverse_ref, *refs):
    others = [ref[...].astype(F32) for ref in refs[:-1]]
    others = jnp.concatenate(others, axis=0).astype(BF16)
    unit = unit_ref[...]
    slopes = slopes_of(unit.astype(BF16), others)
    refs[-1][...] = chain_back(10.0 * nn(slopes, others), unit, inverse_ref[:, :1])


def exchange(array, devices, flip, axis="grp"):
    return lax.ppermute(array, axis, [(i, i ^ flip) for i in range(devices)])


def all_blocks(array, blocks):
    return [array] + [
        lax.ppermute(array, "blk", [(i, (i + by) % blocks) for i in range(blocks)])
        for by in range(1, blocks)
    ]


def exchange_chips(arrays, devices, order):
    return [
        exchange(array, devices, m * CORES + 1) if m else array
        for m, array in zip(order, arrays)
    ]


def local(patches, probe, w_key, w_value, w_out, texts):
    images, patch_count, width = patches.shape
    devices = lax.axis_size("grp")
    blocks = lax.axis_size("blk")
    part = w_key.shape[0]
    heads = HEADS // devices
    scaling = 1.0 / math.sqrt(width // HEADS)
    flat = patches.reshape(images * patch_count, width)

    rows = heads * images
    chips = devices // CORES
    wide = CORES * part
    packed = part // rows * wide
    fit = packed // width

    length = 3 * HEADS // rows * part
    parts = call(
        functools.partial(prepare_kernel, chips),
        [struct((rows, packed + length), BF16)] * chips,
        *[pltpu.with_memory_space_constraint(a, pltpu.HBM) for a in (probe, w_key, w_value)],
        scratch=[
            pltpu.VMEM(probe.shape, BF16),
            pltpu.VMEM(w_key.shape, BF16),
            pltpu.VMEM(w_value.shape, BF16),
            pltpu.VMEM((chips, rows, packed), BF16),
            pltpu.SemaphoreType.DMA((3,)),
        ],
        space=pltpu.HBM,
    )
    parts = exchange_chips(parts, devices, range(chips))
    row, column = struct((images, width), F32), struct((images, 128), F32)
    all_texts = all_blocks(texts, blocks)
    words, unit_text, inverse_text = call(
        functools.partial(unit_text_kernel, blocks),
        (struct((blocks * images, width), BF16), row, column),
        *all_texts,
    )
    keys = call(
        functools.partial(pack_keys_kernel, chips), struct((chips, rows, length), BF16), *parts, all_texts[1]
    )
    shard = call(
        functools.partial(shard_kernel, chips),
        struct((chips + pl.cdiv(part // rows, fit), rows, packed), BF16),
        *parts,
        w_out,
        keys,
    )
    mixed = call(
        functools.partial(attend_kernel, images, scaling, chips),
        [struct((CORES, rows, width), BF16)] * chips,
        flat,
        keys,
        exchange(keys, devices, 1),
        cost=10000000000,
        scratch=[
            pltpu.VMEM((chips, CORES, rows, length), BF16),
            pltpu.VMEM((3 * HEADS, width), BF16),
            pltpu.VMEM((chips, CORES, rows, width), BF16),
        ],
    )
    w_values, w_outs = call(
        functools.partial(unpack_kernel, chips),
        (
            struct((CORES, chips, CORES, part, part), BF16),
            struct((CORES, part, width), BF16),
        ),
        *parts,
        w_out,
        exchange(shard, devices, 1),
    )
    partial_embed = call(
        functools.partial(project_kernel, images, chips),
        [struct((images, width), BF16)] * chips,
        *exchange_chips(mixed, devices, far_first(chips)),
        w_values,
        w_outs,
    )
    unit, inverse, rounded = call(
        functools.partial(unit_image_kernel, chips),
        (row, column, struct((images, width), BF16)),
        *exchange_chips(partial_embed, devices, far_first(chips)),
        inverse_text,
    )
    all_images = [exchange(rounded, blocks, m, "blk") for m in range(blocks - 1, 0, -1)]
    grad_image = call(grad_kernel, row, unit, inverse, words)
    grad_text = call(grad_kernel, row, unit_text, inverse_text, rounded, *all_images)
    return grad_image, grad_text


def solution(mesh):
    in_specs = (
        P(("grp", "blk"), None, None),
        P(),
        P("grp", None),
        P("grp", None),
        P("grp", None),
        P(("grp", "blk"), None),
    )
    out_specs = (P(("grp", "blk"), None), P(("grp", "blk"), None))
    return jax.shard_map(local, mesh=mesh, in_specs=in_specs, out_specs=out_specs, check_vma=False)
```

```python
import functools
import math

import jax
import jax.numpy as jnp
from jax import lax
from jax.experimental import pallas as pl
from jax.experimental.pallas import tpu as pltpu
from jax.sharding import PartitionSpec as P

HEADS = 16
CORES = 2
F32 = jnp.float32
BF16 = jnp.bfloat16


def struct(shape, dtype):
    return jax.ShapeDtypeStruct(shape, dtype)


def call(body, out, *args, scratch=(), space=pltpu.VMEM, cost=None):
    return pl.pallas_call(
        body,
        out_shape=out,
        in_specs=[pl.BlockSpec(memory_space=space)] * len(args),
        scratch_shapes=scratch,
        cost_estimate=cost and pl.CostEstimate(flops=cost, bytes_accessed=0, transcendentals=0),
        compiler_params=pltpu.CompilerParams(vmem_limit_bytes=24 * 2**20),
    )(*args)


def nt(left, right):
    return lax.dot_general(left, right, (((1,), (1,)), ((), ())), preferred_element_type=F32)


def nn(left, right):
    return jnp.dot(left, right, preferred_element_type=F32)


def unit_rows(values):
    inverse = lax.rsqrt(jnp.sum(values * values, axis=1, keepdims=True) + 1e-06)
    return values * inverse, inverse


def chain_back(grad_unit, unit_f, inverse):
    inner = jnp.sum(unit_f * grad_unit, axis=1, keepdims=True)
    return (grad_unit - unit_f * inner) * inverse


def slopes_of(left, right):
    logits = 10.0 * nt(left, right) - 2.0
    row = lax.broadcasted_iota(jnp.int32, logits.shape, 0)
    column = lax.broadcasted_iota(jnp.int32, logits.shape, 1)
    target = jnp.where(row == column, 1.0, 0.0)
    return (jax.nn.sigmoid(logits) - target).astype(BF16)


def split_terms(values):
    high = values.astype(BF16)
    rest = values - high.astype(F32)
    middle = rest.astype(BF16)
    return high, middle, (rest - middle.astype(F32)).astype(BF16)


def far_first(chips):
    return [0, chips - 1, *range(1, chips - 1)]


def chip_and_core():
    place = lax.axis_index("grp")
    return place // CORES, lax.rem(place, CORES)


def prepare_kernel(chips, probe_hbm, w_key_hbm, w_value_hbm, *refs):
    out_refs, (probe, w_key, w_value, blocks, sems) = refs[:chips], refs[chips:]
    part, width = w_key.shape
    _, rows, packed = blocks.shape
    copies = [
        pltpu.make_async_copy(source, target, sems.at[i])
        for i, (source, target) in enumerate(
            [(probe_hbm, probe), (w_key_hbm, w_key), (w_value_hbm, w_value)]
        )
    ]
    for copy in copies:
        copy.start()
    head = lax.broadcasted_iota(jnp.int32, (HEADS, width), 0)
    first = lax.broadcasted_iota(jnp.int32, (HEADS, width), 1) - head * (width // HEADS)
    inside = (first >= 0) & (first < width // HEADS)
    copies[0].wait()
    table = jnp.where(inside, probe[...].astype(F32).reshape(1, width), 0.0).astype(BF16)
    copies[1].wait()
    keys = [
        term[h * rows : (h + 1) * rows]
        for term in split_terms(nt(table, w_key[...]))
        for h in range(HEADS // rows)
    ]
    keys = jnp.concatenate(keys, axis=1)
    copies[2].wait()
    wide = width // chips
    for q in range(chips):
        columns = w_value[:, q * wide : (q + 1) * wide]
        pieces = [columns[j * rows : (j + 1) * rows] for j in range(part // rows)]
        blocks[q] = jnp.concatenate(pieces, axis=1)
    chip, _ = chip_and_core()
    for m, out_ref in enumerate(out_refs):
        out_ref[:, :packed] = blocks[chip ^ m]
        out_ref[:, packed:] = keys


def pack_keys_kernel(chips, *refs):
    length = refs[-1].shape[2]
    for m in range(chips):
        refs[-1][m] = refs[m][:, refs[m].shape[1] - length :]


def turn_kernel(x_ref, _, out_ref):
    out_ref[...] = x_ref[...].T


def shard_kernel(chips, *refs):
    w_out_ref, _, out_ref = refs[chips:]
    _, rows, length = out_ref.shape
    part, width = w_out_ref.shape
    for m in range(chips):
        out_ref[m] = refs[m][:, :length]
    fit = length // width
    for j in range(part // rows):
        first = j % fit * width
        out_ref[chips + j // fit, :, first : first + width] = w_out_ref[j * rows : (j + 1) * rows]


def attend_kernel(images, scaling, chips, x_ref, own_ref, other_ref, *refs):
    outs, (placed, table, every) = refs[:chips], refs[chips:]
    x = x_ref[...]
    width = x.shape[1]
    patches = x.shape[0] // images
    _, rows, length = own_ref.shape
    part = width // (chips * CORES)
    chip, core = chip_and_core()
    for m in range(chips):
        place = core if m == 0 else 1 - core
        placed[chip ^ m, place] = own_ref[m]
        placed[chip ^ m, 1 - place] = other_ref[m]
    for j in range(length // part):
        for k in range(chips * CORES):
            table[j * rows : (j + 1) * rows, k * part : (k + 1) * part] = placed[
                k // CORES, k % CORES, :, j * part : (j + 1) * part
            ]
    parts = nt(table[...], x)
    scores = (parts[:HEADS] + parts[HEADS : 2 * HEADS] + parts[2 * HEADS :]) * scaling
    image = lax.broadcasted_iota(jnp.int32, (images, x.shape[0]), 0)
    first = lax.broadcasted_iota(jnp.int32, (images, x.shape[0]), 1) - image * patches
    own = (first >= 0) & (first < patches)
    spread = jnp.where(own[None], scores[:, None, :], -jnp.inf)
    expo = jnp.exp(spread - jnp.max(spread, axis=2, keepdims=True))
    weights = expo / jnp.sum(expo, axis=2, keepdims=True)
    weights = weights.reshape(HEADS * images, x.shape[0])
    every[...] = weights.astype(BF16).reshape(every.shape)
    ordered = jnp.concatenate([every[chip ^ m] for m in far_first(chips)], axis=0)
    mixed = nn(ordered, x).astype(BF16).reshape(chips, *outs[0].shape)
    for i, out_ref in enumerate(outs):
        out_ref[...] = mixed[i]


def unpack_kernel(chips, *refs):
    w_out_ref, other_ref, w_value_ref, outs_ref = refs[chips:]
    part, width = w_out_ref.shape
    rows = other_ref.shape[1]
    chip, core = chip_and_core()
    for m in range(chips):
        for c, source in enumerate((refs[m], other_ref.at[m])):
            place = core if (c == 0) == (m == 0) else 1 - core
            for t in range(CORES):
                for j in range(part // rows):
                    first = (j * CORES + t) * part
                    w_value_ref[t, chip ^ m, place, j * rows : (j + 1) * rows] = source[
                        :, first : first + part
                    ]
    outs_ref[core] = w_out_ref[...]
    fit = other_ref.shape[2] // width
    for j in range(part // rows):
        first = j % fit * width
        outs_ref[1 - core, j * rows : (j + 1) * rows] = other_ref[
            chips + j // fit, :, first : first + width
        ]


def project_kernel(images, chips, *refs):
    mixed_refs, (w_value_ref, outs_ref), out_refs = refs[:chips], refs[chips : chips + 2], refs[chips + 2 :]
    _, rows, width = mixed_refs[0].shape
    part = outs_ref.shape[1]
    heads = rows // images
    head = lax.broadcasted_iota(jnp.int32, (chips, images, part), 2)
    embed = jnp.zeros((chips * images, width), F32)
    for t in range(CORES):
        mixed = jnp.concatenate([ref[t] for ref in mixed_refs], axis=0)
        every = nn(mixed, w_value_ref[t].reshape(width, part))
        every = every.reshape(chips, heads, images, part)
        pooled = every[:, 0]
        for h in range(1, heads):
            pooled = jnp.where(head >= h * (part // heads), every[:, h], pooled)
        pooled = pooled.reshape(chips * images, part).astype(BF16)
        embed = embed + nn(pooled, outs_ref[t])
    for m, out_ref in enumerate(out_refs):
        out_ref[...] = embed[m * images : (m + 1) * images].astype(BF16)


def unit_text_kernel(blocks, *refs):
    words_ref, unit_ref, inverse_ref = refs[blocks:]
    images = unit_ref.shape[0]
    texts = jnp.concatenate([ref[...].astype(F32) for ref in refs[:blocks]], axis=0)
    units, inverses = unit_rows(texts)
    words_ref[...] = units.astype(BF16)
    unit_ref[...] = units[:images]
    inverse_ref[...] = jnp.broadcast_to(inverses[:images], inverse_ref.shape)


def unit_image_kernel(chips, *refs):
    unit_ref, inverse_ref, rounded_ref = refs[chips + 1 :]
    embed = refs[0][...].astype(F32)
    for ref in refs[1:chips]:
        embed = embed + ref[...].astype(F32)
    unit, inverse = unit_rows(embed)
    unit_ref[...] = unit
    inverse_ref[...] = jnp.broadcast_to(inverse, inverse_ref.shape)
    rounded_ref[...] = unit.astype(BF16)


def grad_kernel(unit_ref, inverse_ref, *refs):
    others = [ref[...].astype(F32) for ref in refs[:-1]]
    others = jnp.concatenate(others, axis=0).astype(BF16)
    unit = unit_ref[...]
    slopes = slopes_of(unit.astype(BF16), others)
    refs[-1][...] = chain_back(10.0 * nn(slopes, others), unit, inverse_ref[:, :1])


def exchange(array, devices, flip, axis="grp"):
    return lax.ppermute(array, axis, [(i, i ^ flip) for i in range(devices)])


def all_blocks(array, blocks):
    return [array] + [
        lax.ppermute(array, "blk", [(i, (i + by) % blocks) for i in range(blocks)])
        for by in range(1, blocks)
    ]


def exchange_chips(arrays, devices, order):
    return [
        exchange(array, devices, m * CORES + 1) if m else array
        for m, array in zip(order, arrays)
    ]


def local(patches, probe, w_key, w_value, w_out, texts):
    images, patch_count, width = patches.shape
    devices = lax.axis_size("grp")
    blocks = lax.axis_size("blk")
    part = w_key.shape[0]
    heads = HEADS // devices
    scaling = 1.0 / math.sqrt(width // HEADS)
    flat = patches.reshape(images * patch_count, width)

    rows = heads * images
    chips = devices // CORES
    wide = CORES * part
    packed = part // rows * wide
    fit = packed // width

    length = 3 * HEADS // rows * part
    parts = call(
        functools.partial(prepare_kernel, chips),
        [struct((rows, packed + length), BF16)] * chips,
        *[pltpu.with_memory_space_constraint(a, pltpu.HBM) for a in (probe, w_key, w_value)],
        scratch=[
            pltpu.VMEM(probe.shape, BF16),
            pltpu.VMEM(w_key.shape, BF16),
            pltpu.VMEM(w_value.shape, BF16),
            pltpu.VMEM((chips, rows, packed), BF16),
            pltpu.SemaphoreType.DMA((3,)),
        ],
        space=pltpu.HBM,
    )
    parts = exchange_chips(parts, devices, range(chips))
    keys = call(
        functools.partial(pack_keys_kernel, chips), struct((chips, rows, length), BF16), *parts
    )
    shard = call(
        functools.partial(shard_kernel, chips),
        struct((chips + pl.cdiv(part // rows, fit), rows, packed), BF16),
        *parts,
        w_out,
        keys,
    )
    mixed = call(
        functools.partial(attend_kernel, images, scaling, chips),
        [struct((CORES, rows, width), BF16)] * chips,
        flat,
        keys,
        exchange(keys, devices, 1),
        cost=10000000000,
        scratch=[
            pltpu.VMEM((chips, CORES, rows, length), BF16),
            pltpu.VMEM((3 * HEADS, width), BF16),
            pltpu.VMEM((chips, CORES * rows, flat.shape[0]), BF16),
        ],
    )
    w_values, w_outs = call(
        functools.partial(unpack_kernel, chips),
        (
            struct((CORES, chips, CORES, part, part), BF16),
            struct((CORES, part, width), BF16),
        ),
        *parts,
        w_out,
        exchange(shard, devices, 1),
    )
    partial_embed = call(
        functools.partial(project_kernel, images, chips),
        [struct((images, width), BF16)] * chips,
        *exchange_chips(mixed, devices, far_first(chips)),
        w_values,
        w_outs,
    )
    row, column = struct((images, width), F32), struct((images, 128), F32)
    words, unit_text, inverse_text = call(
        functools.partial(unit_text_kernel, blocks),
        (struct((blocks * images, width), BF16), row, column),
        *all_blocks(texts, blocks),
    )
    unit, inverse, rounded = call(
        functools.partial(unit_image_kernel, chips),
        (row, column, struct((images, width), BF16)),
        *exchange_chips(partial_embed, devices, far_first(chips)),
        inverse_text,
    )
    all_images = [exchange(rounded, blocks, m, "blk") for m in range(blocks - 1, 0, -1)]
    grad_image = call(grad_kernel, row, unit, inverse, words)
    grad_text = call(grad_kernel, row, unit_text, inverse_text, rounded, *all_images)
    return grad_image, grad_text


def solution(mesh):
    in_specs = (
        P(("grp", "blk"), None, None),
        P(),
        P("grp", None),
        P("grp", None),
        P("grp", None),
        P(("grp", "blk"), None),
    )
    out_specs = (P(("grp", "blk"), None), P(("grp", "blk"), None))
    return jax.shard_map(local, mesh=mesh, in_specs=in_specs, out_specs=out_specs, check_vma=False)
```

```python
import functools
import math

import jax
import jax.numpy as jnp
from jax import lax
from jax.experimental import pallas as pl
from jax.experimental.pallas import tpu as pltpu
from jax.sharding import PartitionSpec as P

HEADS = 16
CORES = 2
F32 = jnp.float32
BF16 = jnp.bfloat16


def struct(shape, dtype):
    return jax.ShapeDtypeStruct(shape, dtype)


def call(body, out, *args, scratch=(), space=pltpu.VMEM, cost=None):
    return pl.pallas_call(
        body,
        out_shape=out,
        in_specs=[pl.BlockSpec(memory_space=space)] * len(args),
        scratch_shapes=scratch,
        cost_estimate=cost and pl.CostEstimate(flops=cost, bytes_accessed=0, transcendentals=0),
        compiler_params=pltpu.CompilerParams(vmem_limit_bytes=24 * 2**20),
    )(*args)


def nt(left, right):
    return lax.dot_general(left, right, (((1,), (1,)), ((), ())), preferred_element_type=F32)


def nn(left, right):
    return jnp.dot(left, right, preferred_element_type=F32)


def unit_rows(values):
    inverse = lax.rsqrt(jnp.sum(values * values, axis=1, keepdims=True) + 1e-06)
    return values * inverse, inverse


def chain_back(grad_unit, unit_f, inverse):
    inner = jnp.sum(unit_f * grad_unit, axis=1, keepdims=True)
    return (grad_unit - unit_f * inner) * inverse


def slopes_of(left, right):
    logits = 10.0 * nt(left, right) - 2.0
    row = lax.broadcasted_iota(jnp.int32, logits.shape, 0)
    column = lax.broadcasted_iota(jnp.int32, logits.shape, 1)
    target = jnp.where(row == column, 1.0, 0.0)
    return (jax.nn.sigmoid(logits) - target).astype(BF16)


def split_terms(values):
    high = values.astype(BF16)
    rest = values - high.astype(F32)
    middle = rest.astype(BF16)
    return high, middle, (rest - middle.astype(F32)).astype(BF16)


def near_first(chips):
    return list(range(chips))


def chip_and_core():
    place = lax.axis_index("grp")
    return place // CORES, lax.rem(place, CORES)


def prepare_kernel(chips, probe_hbm, w_key_hbm, w_value_hbm, *refs):
    out_refs, (probe, w_key, w_value, blocks, sems) = refs[:chips], refs[chips:]
    part, width = w_key.shape
    _, rows, packed = blocks.shape
    copies = [
        pltpu.make_async_copy(source, target, sems.at[i])
        for i, (source, target) in enumerate(
            [(probe_hbm, probe), (w_key_hbm, w_key), (w_value_hbm, w_value)]
        )
    ]
    for copy in copies:
        copy.start()
    head = lax.broadcasted_iota(jnp.int32, (HEADS, width), 0)
    first = lax.broadcasted_iota(jnp.int32, (HEADS, width), 1) - head * (width // HEADS)
    inside = (first >= 0) & (first < width // HEADS)
    copies[0].wait()
    table = jnp.where(inside, probe[...].astype(F32).reshape(1, width), 0.0).astype(BF16)
    copies[1].wait()
    keys = [
        term[h * rows : (h + 1) * rows]
        for term in split_terms(nt(table, w_key[...]))
        for h in range(HEADS // rows)
    ]
    keys = jnp.concatenate(keys, axis=1)
    copies[2].wait()
    wide = width // chips
    for q in range(chips):
        columns = w_value[:, q * wide : (q + 1) * wide]
        pieces = [columns[j * rows : (j + 1) * rows] for j in range(part // rows)]
        blocks[q] = jnp.concatenate(pieces, axis=1)
    chip, _ = chip_and_core()
    for m, out_ref in enumerate(out_refs):
        out_ref[:, :packed] = blocks[chip ^ m]
        out_ref[:, packed:] = keys


def pack_keys_kernel(chips, *refs):
    length = refs[-1].shape[2]
    for m in range(chips):
        refs[-1][m] = refs[m][:, refs[m].shape[1] - length :]


def turn_kernel(x_ref, _, out_ref):
    out_ref[...] = x_ref[...].T


def shard_kernel(chips, *refs):
    w_out_ref, _, out_ref = refs[chips:]
    _, rows, length = out_ref.shape
    part, width = w_out_ref.shape
    for m in range(chips):
        out_ref[m] = refs[m][:, :length]
    fit = length // width
    for j in range(part // rows):
        first = j % fit * width
        out_ref[chips + j // fit, :, first : first + width] = w_out_ref[j * rows : (j + 1) * rows]


def attend_kernel(images, scaling, chips, x_ref, own_ref, other_ref, *refs):
    outs, (placed, table, every) = refs[:chips], refs[chips:]
    x = x_ref[...]
    width = x.shape[1]
    patches = x.shape[0] // images
    _, rows, length = own_ref.shape
    part = width // (chips * CORES)
    chip, core = chip_and_core()
    for m in range(chips):
        place = core if m == 0 else 1 - core
        placed[chip ^ m, place] = own_ref[m]
        placed[chip ^ m, 1 - place] = other_ref[m]
    for j in range(length // part):
        for k in range(chips * CORES):
            table[j * rows : (j + 1) * rows, k * part : (k + 1) * part] = placed[
                k // CORES, k % CORES, :, j * part : (j + 1) * part
            ]
    parts = nt(table[...], x)
    scores = (parts[:HEADS] + parts[HEADS : 2 * HEADS] + parts[2 * HEADS :]) * scaling
    image = lax.broadcasted_iota(jnp.int32, (images, x.shape[0]), 0)
    first = lax.broadcasted_iota(jnp.int32, (images, x.shape[0]), 1) - image * patches
    own = (first >= 0) & (first < patches)
    spread = jnp.where(own[None], scores[:, None, :], -jnp.inf)
    expo = jnp.exp(spread - jnp.max(spread, axis=2, keepdims=True))
    weights = expo / jnp.sum(expo, axis=2, keepdims=True)
    weights = weights.reshape(HEADS * images, x.shape[0])
    every[...] = nn(weights.astype(BF16), x).astype(BF16).reshape(every.shape)
    for m, out_ref in zip(near_first(chips), outs):
        out_ref[...] = every[chip ^ m]


def unpack_kernel(chips, *refs):
    w_out_ref, other_ref, w_value_ref, outs_ref = refs[chips:]
    part, width = w_out_ref.shape
    rows = other_ref.shape[1]
    chip, core = chip_and_core()
    for m in range(chips):
        for c, source in enumerate((refs[m], other_ref.at[m])):
            place = core if (c == 0) == (m == 0) else 1 - core
            for t in range(CORES):
                for j in range(part // rows):
                    first = (j * CORES + t) * part
                    w_value_ref[t, chip ^ m, place, j * rows : (j + 1) * rows] = source[
                        :, first : first + part
                    ]
    outs_ref[core] = w_out_ref[...]
    fit = other_ref.shape[2] // width
    for j in range(part // rows):
        first = j % fit * width
        outs_ref[1 - core, j * rows : (j + 1) * rows] = other_ref[
            chips + j // fit, :, first : first + width
        ]


def project_kernel(images, chips, *refs):
    mixed_refs, (w_value_ref, outs_ref), out_refs = refs[:chips], refs[chips : chips + 2], refs[chips + 2 :]
    _, rows, width = mixed_refs[0].shape
    part = outs_ref.shape[1]
    heads = rows // images
    head = lax.broadcasted_iota(jnp.int32, (chips, images, part), 2)
    embed = jnp.zeros((chips * images, width), F32)
    for t in range(CORES):
        mixed = jnp.concatenate([ref[t] for ref in mixed_refs], axis=0)
        every = nn(mixed, w_value_ref[t].reshape(width, part))
        every = every.reshape(chips, heads, images, part)
        pooled = every[:, 0]
        for h in range(1, heads):
            pooled = jnp.where(head >= h * (part // heads), every[:, h], pooled)
        pooled = pooled.reshape(chips * images, part).astype(BF16)
        embed = embed + nn(pooled, outs_ref[t])
    for m, out_ref in enumerate(out_refs):
        out_ref[...] = embed[m * images : (m + 1) * images].astype(BF16)


def unit_text_kernel(blocks, *refs):
    words_ref, unit_ref, inverse_ref = refs[blocks:]
    images = unit_ref.shape[0]
    texts = jnp.concatenate([ref[...].astype(F32) for ref in refs[:blocks]], axis=0)
    units, inverses = unit_rows(texts)
    words_ref[...] = units.astype(BF16)
    unit_ref[...] = units[:images]
    inverse_ref[...] = jnp.broadcast_to(inverses[:images], inverse_ref.shape)


def unit_image_kernel(chips, *refs):
    unit_ref, inverse_ref, rounded_ref = refs[chips + 1 :]
    embed = refs[0][...].astype(F32)
    for ref in refs[1:chips]:
        embed = embed + ref[...].astype(F32)
    unit, inverse = unit_rows(embed)
    unit_ref[...] = unit
    inverse_ref[...] = jnp.broadcast_to(inverse, inverse_ref.shape)
    rounded_ref[...] = unit.astype(BF16)


def grad_kernel(unit_ref, inverse_ref, *refs):
    others = [ref[...].astype(F32) for ref in refs[:-1]]
    others = jnp.concatenate(others, axis=0).astype(BF16)
    unit = unit_ref[...]
    slopes = slopes_of(unit.astype(BF16), others)
    refs[-1][...] = chain_back(10.0 * nn(slopes, others), unit, inverse_ref[:, :1])


def exchange(array, devices, flip, axis="grp"):
    return lax.ppermute(array, axis, [(i, i ^ flip) for i in range(devices)])


def all_blocks(array, blocks):
    return [array] + [
        lax.ppermute(array, "blk", [(i, (i + by) % blocks) for i in range(blocks)])
        for by in range(1, blocks)
    ]


def exchange_chips(arrays, devices, order):
    return [
        exchange(array, devices, m * CORES + 1) if m else array
        for m, array in zip(order, arrays)
    ]


def local(patches, probe, w_key, w_value, w_out, texts):
    images, patch_count, width = patches.shape
    devices = lax.axis_size("grp")
    blocks = lax.axis_size("blk")
    part = w_key.shape[0]
    heads = HEADS // devices
    scaling = 1.0 / math.sqrt(width // HEADS)
    flat = patches.reshape(images * patch_count, width)

    rows = heads * images
    chips = devices // CORES
    wide = CORES * part
    packed = part // rows * wide
    fit = packed // width

    length = 3 * HEADS // rows * part
    parts = call(
        functools.partial(prepare_kernel, chips),
        [struct((rows, packed + length), BF16)] * chips,
        *[pltpu.with_memory_space_constraint(a, pltpu.HBM) for a in (probe, w_key, w_value)],
        scratch=[
            pltpu.VMEM(probe.shape, BF16),
            pltpu.VMEM(w_key.shape, BF16),
            pltpu.VMEM(w_value.shape, BF16),
            pltpu.VMEM((chips, rows, packed), BF16),
            pltpu.SemaphoreType.DMA((3,)),
        ],
        space=pltpu.HBM,
    )
    parts = exchange_chips(parts, devices, range(chips))
    row, column = struct((images, width), F32), struct((images, 128), F32)
    all_texts = all_blocks(texts, blocks)
    words, unit_text, inverse_text = call(
        functools.partial(unit_text_kernel, blocks),
        (struct((blocks * images, width), BF16), row, column),
        *all_texts,
    )
    keys = call(
        functools.partial(pack_keys_kernel, chips), struct((chips, rows, length), BF16), *parts, all_texts[1]
    )
    shard = call(
        functools.partial(shard_kernel, chips),
        struct((chips + pl.cdiv(part // rows, fit), rows, packed), BF16),
        *parts,
        w_out,
        keys,
    )
    mixed = call(
        functools.partial(attend_kernel, images, scaling, chips),
        [struct((CORES, rows, width), BF16)] * chips,
        flat,
        keys,
        exchange(keys, devices, 1),
        cost=10000000000,
        scratch=[
            pltpu.VMEM((chips, CORES, rows, length), BF16),
            pltpu.VMEM((3 * HEADS, width), BF16),
            pltpu.VMEM((chips, CORES, rows, width), BF16),
        ],
    )
    w_values, w_outs = call(
        functools.partial(unpack_kernel, chips),
        (
            struct((CORES, chips, CORES, part, part), BF16),
            struct((CORES, part, width), BF16),
        ),
        *parts,
        w_out,
        exchange(shard, devices, 1),
    )
    partial_embed = call(
        functools.partial(project_kernel, images, chips),
        [struct((images, width), BF16)] * chips,
        *exchange_chips(mixed, devices, near_first(chips)),
        w_values,
        w_outs,
    )
    unit, inverse, rounded = call(
        functools.partial(unit_image_kernel, chips),
        (row, column, struct((images, width), BF16)),
        *exchange_chips(partial_embed, devices, near_first(chips)),
        inverse_text,
    )
    all_images = [exchange(rounded, blocks, m, "blk") for m in range(blocks - 1, 0, -1)]
    grad_image = call(grad_kernel, row, unit, inverse, words)
    grad_text = call(grad_kernel, row, unit_text, inverse_text, rounded, *all_images)
    return grad_image, grad_text


def solution(mesh):
    in_specs = (
        P(("grp", "blk"), None, None),
        P(),
        P("grp", None),
        P("grp", None),
        P("grp", None),
        P(("grp", "blk"), None),
    )
    out_specs = (P(("grp", "blk"), None), P(("grp", "blk"), None))
    return jax.shard_map(local, mesh=mesh, in_specs=in_specs, out_specs=out_specs, check_vma=False)
```
